32 devices in a mesh: tm: 16 (over z, y, x), run: 2 (over core).
Axes of the slice: x: 2, y: 2, z: 4, core: 2. Of those that a mesh axis runs over, the one named last changes fastest.
Arguments:
- signal: bfloat16 [2, 16384, 256], P('run', 'tm'), may hold values from -6 to 6
- conv_weight: bfloat16 [768, 512], replicated, may hold values from -0.21875 to 0.21875
- conv_bias: float32 [512], replicated, may hold values from -3 to 3
- out_weight: bfloat16 [256, 256], replicated, may hold values from -0.375 to 0.375
- out_bias: float32 [256], replicated, may hold values from -3 to 3
- cotangent: bfloat16 [2, 16384, 256], P('run', 'tm'), may hold values from -8 to 8
Outputs:
- output: bfloat16 [2, 16384, 256], P('run', 'tm')
- grad_signal: bfloat16 [2, 16384, 256], P('run', 'tm')
- grad_conv_weight: float32 [768, 512], replicated
- grad_conv_bias: float32 [512], replicated
- grad_out_weight: float32 [256, 256], replicated
- grad_out_bias: float32 [256], replicated
The draws below stay inside these ranges and needn't reach their ends.
All inputs are finite; a program needn't handle non-finite values.
Results may differ from the reference program's by a relative error of at most 0.0034.
Values may be sent and summed in bfloat16 or wider, within the bound.
No kernel may reach another device: no remote copies, remote signals or barrier semaphores. Data moves between devices by JAX's collectives and lax.ppermute only.
A program may use at most 64 MiB of HBM per device.

```python
import jax
import jax.numpy as jnp
from jax import lax

C = 256
DILATION_STEPS = 256
KERNEL_TAPS = 3
STEPS = 16384
RUNS = 2


def draw_cotangent(key, part):
    key_base = jax.random.fold_in(key, 0)
    position = jnp.arange(STEPS, dtype=jnp.float32) / max(STEPS - 1, 1)
    ramp = jnp.exp(jnp.log(3.0) * (position - 0.5))[None, :, None]
    values = jax.random.normal(key_base, (RUNS, STEPS, C), jnp.float32) * ramp
    return jnp.clip(values, -8.0, 8.0).astype(jnp.bfloat16)


def level_of(own_key, shape, shards, low, high):
    loudness, own = 1.0, jax.random.fold_in(own_key, 6)
    for dim, parts in shards:
        heights = jnp.exp(jax.random.uniform(jax.random.fold_in(own, dim), (parts,), jnp.float32, low / len(shards), high / len(shards)))
        loudness = loudness * jnp.repeat(heights, shape[dim] // parts).reshape([-1 if axis == dim else 1 for axis in range(len(shape))])
    return loudness


def normal_values(key, dims, width, reach, cuts=(), kind=jnp.bfloat16):
    level = level_of(key, dims, cuts, -0.22, 0.18) if cuts else 1.0
    values = jax.random.normal(key, dims, jnp.float32) * width * level
    return jnp.minimum(jnp.maximum(values, -reach), reach).astype(kind)


def setup_inputs(seed: int = 0) -> dict:
    arg_keys = jax.random.split(jax.random.key(seed), 7)
    return {
        "signal": normal_values(arg_keys[0], (RUNS, STEPS, C), 1.0, 6.0, ((0, 2), (1, 16))),
        "conv_weight": normal_values(arg_keys[1], (KERNEL_TAPS * C, 2 * C), (KERNEL_TAPS * C) ** -0.5, 0.21875),
        "conv_bias": normal_values(arg_keys[2], (2 * C,), 0.5, 3.0, (), jnp.float32),
        "out_weight": normal_values(arg_keys[3], (C, C), C ** -0.5, 0.375),
        "out_bias": normal_values(arg_keys[4], (C,), 0.5, 3.0, (), jnp.float32),
        "cotangent": draw_cotangent(jax.random.fold_in(arg_keys[6], 71), 0),
    }


def reference(signal, conv_weight, conv_bias, out_weight, out_bias, cotangent):
    receptive_span = (KERNEL_TAPS - 1) * DILATION_STEPS

    def one_run(pair):
        signal_run, cot_run = pair
        total_steps = signal_run.shape[0]
        padded_input = jnp.concatenate([jnp.zeros((receptive_span, C), signal_run.dtype), signal_run], 0)
        tap_stack = jnp.concatenate([padded_input[receptive_span - kernel_tap_index * DILATION_STEPS: receptive_span - kernel_tap_index * DILATION_STEPS + total_steps] for kernel_tap_index in range(KERNEL_TAPS)], 1)
        preact = jnp.dot(tap_stack, conv_weight, preferred_element_type=jnp.float32) + conv_bias
        filtered = jnp.tanh(preact[:, :C])
        gated = jax.nn.sigmoid(preact[:, C:])
        mixed = (filtered * gated).astype(jnp.bfloat16)
        hidden = jnp.dot(mixed, out_weight, preferred_element_type=jnp.float32) + out_bias
        output = (signal_run.astype(jnp.float32) + hidden).astype(jnp.bfloat16)
        dmixed = jnp.dot(cot_run, out_weight.T, preferred_element_type=jnp.float32)
        dpre = jnp.concatenate([dmixed * gated * (1.0 - filtered * filtered), dmixed * filtered * gated * (1.0 - gated)], 1).astype(jnp.bfloat16)
        dstacked = jnp.dot(dpre, conv_weight.T, preferred_element_type=jnp.float32)
        padded_input_gradient = jnp.zeros((receptive_span + total_steps, C), jnp.float32)
        for kernel_tap_index in range(KERNEL_TAPS):
            shifted_slice = dstacked[:, kernel_tap_index * C:(kernel_tap_index + 1) * C]
            padded_input_gradient = padded_input_gradient + jnp.pad(shifted_slice, ((receptive_span - kernel_tap_index * DILATION_STEPS, kernel_tap_index * DILATION_STEPS), (0, 0)))
        grad_run = (cot_run.astype(jnp.float32) + padded_input_gradient[receptive_span:]).astype(jnp.bfloat16)
        grads = (jnp.dot(tap_stack.T, dpre, preferred_element_type=jnp.float32),
                 jnp.sum(dpre.astype(jnp.float32), 0),
                 jnp.dot(mixed.T, cot_run, preferred_element_type=jnp.float32),
                 jnp.sum(cot_run.astype(jnp.float32), 0))
        return output, grad_run, grads

    outputs, grad_signal, grads = lax.map(one_run, (signal, cotangent))
    scale = float(RUNS * STEPS) ** -0.5
    return (outputs, grad_signal, jnp.sum(grads[0], 0) * scale, jnp.sum(grads[1], 0) * scale,
            jnp.sum(grads[2], 0) * scale, jnp.sum(grads[3], 0) * scale)
```

```python
import functools

import jax
import jax.numpy as jnp
from jax import lax
from jax.experimental import pallas as pl
from jax.experimental.pallas import tpu as pltpu
from jax.sharding import PartitionSpec as P

STEP = 256
TAPS = 3
SPAN = (TAPS - 1) * STEP
BOTH = ("tm", "run")
LANES = 128
SUBLANES = 8
BIAS_ROWS = 2 * SUBLANES
F32 = jnp.float32
BF16 = jnp.bfloat16
VMEM = pl.BlockSpec(memory_space=pltpu.VMEM)
SMEM = pl.BlockSpec(memory_space=pltpu.SMEM)
LIMIT = 24 * 1024 * 1024


def call(kernel, out_shape, args, scalars=0, flops=0, scratch=()):
    moved = sum(a.size * a.dtype.itemsize for a in args)
    return pl.pallas_call(
        kernel,
        out_shape=out_shape,
        in_specs=[SMEM] * scalars + [VMEM] * (len(args) - scalars),
        out_specs=[VMEM] * len(out_shape),
        scratch_shapes=list(scratch),
        cost_estimate=pl.CostEstimate(flops=flops, bytes_accessed=moved, transcendentals=0),
        compiler_params=pltpu.CompilerParams(vmem_limit_bytes=LIMIT),
    )(*args)


def shape(dtype, *dims):
    return jax.ShapeDtypeStruct(dims, dtype)


def dot(a, b):
    return jnp.dot(a, b, preferred_element_type=F32)


def dot_rows(a, b):
    return lax.dot_general(a, b, (((0,), (0,)), ((), ())), preferred_element_type=F32)


def dot_columns(a, b):
    return lax.dot_general(a, b, (((1,), (1,)), ((), ())), preferred_element_type=F32)


def gates(preact, dmixed):
    channels = dmixed.shape[1]
    filtered = jnp.tanh(preact[:, :channels])
    gated = jax.nn.sigmoid(preact[:, channels:])
    mixed = filtered * gated
    dfiltered = dmixed * gated * (1.0 - filtered * filtered)
    dgated = dmixed * mixed * (1.0 - gated)
    return mixed.astype(BF16), dfiltered.astype(BF16), dgated.astype(BF16)


def late_kernel(
    signal, weight, bias, out_weight, cot,
    preact_out, dmixed_out, mixed_out, dpre_out, grad_conv, grad_proj, grad_bias,
):
    rows, channels = signal.shape
    tap = lambda k: weight[k * channels : (k + 1) * channels, :]
    preact_out[...] = dot(signal[:SPAN, :], tap(0)) + bias[...]
    for k in range(1, TAPS - 1):
        preact_out[k * STEP :, :] += dot(signal[: SPAN - k * STEP, :], tap(k))
    dmixed_out[...] = dot_columns(cot[:SPAN, :], out_weight[...])
    for begin in range(SPAN, rows, STEP):
        here = slice(begin, begin + STEP)
        at = slice(begin - SPAN, begin - SPAN + STEP)
        preact = bias[...]
        for k in range(TAPS):
            preact = preact + dot(signal[begin - k * STEP : begin - k * STEP + STEP, :], tap(k))
        mixed, dfiltered, dgated = gates(preact, dot_columns(cot[here, :], out_weight[...]))
        mixed_out[at, :] = mixed
        dpre_out[at, :channels] = dfiltered
        dpre_out[at, channels:] = dgated
    dpre = dpre_out[...]
    for k in range(TAPS):
        grad_conv[k * channels : (k + 1) * channels, :] = dot_rows(
            signal[SPAN - k * STEP : rows - k * STEP, :], dpre
        )
    grad_proj[...] = dot_rows(mixed_out[...], cot[SPAN:, :])
    ones = jnp.ones((BIAS_ROWS, rows), BF16)
    grad_bias[:, : 2 * channels] = dot(ones[:, : rows - SPAN], dpre)[:SUBLANES]
    grad_bias[:, 2 * channels :] = dot(ones, cot[...])[:SUBLANES]


def early_kernel(
    fine, first, history, signal, weight, cot, preact_in, dmixed_in, conv_in, proj_in, bias_in,
    mixed_out, dpre_out, main_out, bias_out, message, past, grad_conv, grad_proj,
):
    rows, channels = signal.shape
    tap = lambda k: weight[k * channels : (k + 1) * channels, :]
    past[...] = jnp.where(first[0] == 1, jnp.zeros_like(history), history[...])
    for begin in range(0, SPAN, STEP):
        here = slice(begin, begin + STEP)
        preact = preact_in[here, :]
        for k in range(begin // STEP + 1, TAPS):
            source = SPAN + begin - k * STEP
            preact = preact + dot(past[source : source + STEP, :], tap(k))
        mixed, dfiltered, dgated = gates(preact, dmixed_in[here, :])
        mixed_out[here, :] = mixed
        dpre_out[here, :channels] = dfiltered
        dpre_out[here, channels:] = dgated
    dpre = dpre_out[...]
    for k in range(TAPS):
        at = slice(k * channels, (k + 1) * channels)
        total = conv_in[at, :] + dot_rows(past[SPAN - k * STEP :, :], dpre[: k * STEP, :]) if k else conv_in[at, :]
        if k < TAPS - 1:
            total = total + dot_rows(signal[: SPAN - k * STEP, :], dpre[k * STEP :, :])
        grad_conv[at, :] = total
    grad_proj[...] = proj_in[...] + dot_rows(mixed_out[...], cot[:SPAN, :])
    ones = jnp.ones((BIAS_ROWS, SPAN), BF16)
    columns = dot(ones, dpre)[:SUBLANES]
    bias = bias_in[...]
    bias = jnp.concatenate([bias[:, : 2 * channels] + columns, bias[:, 2 * channels :]], 1)
    lines = [bias[:1, c : c + LANES] for c in range(0, bias.shape[1], LANES)]
    lines += [jnp.zeros((1, LANES), F32)] * (SUBLANES - len(lines))
    bias = jnp.concatenate(lines, 0)
    bias_out[...] = bias
    pieces = main_out.shape[0] // fine
    for piece in range(pieces):
        at = piece * fine
        for grad in (grad_conv, grad_proj):
            height = piece_height(grad.shape[0], pieces)
            begin = piece * height
            count = min(height, grad.shape[0] - begin)
            for column in range(0, grad.shape[1], LANES):
                if count > 0:
                    block = grad[begin : begin + count, column : column + LANES]
                    main_out[at : at + count, :] = block
                    message[at : at + count, :] = block.astype(BF16)
                    padded = at + count
                else:
                    padded = at
                if count < height:
                    blank = jnp.zeros((at + height - padded, LANES), F32)
                    main_out[padded : at + height, :] = blank
                    message[padded : at + height, :] = blank.astype(BF16)
                at += height
    message[pieces * fine :, :] = narrowed(bias)


def back_kernel(dpre, weight, out):
    channels = out.shape[1]
    tap = lambda k: weight[k * channels : (k + 1) * channels, :]
    for begin in range(0, SPAN, STEP):
        total = dot_columns(dpre[begin : begin + STEP, :], tap(TAPS - 1))
        for k in range(1, TAPS - 1):
            source = begin - SPAN + k * STEP
            if source >= 0:
                total = total + dot_columns(dpre[source : source + STEP, :], tap(k))
        out[begin : begin + STEP, :] = total.astype(BF16)


def own_kernel(signal, weight, out_weight, out_bias, cot, mixed_early, mixed_late, dpre_early, dpre_late, output, partial):
    rows, channels = signal.shape
    tap = lambda k: weight[k * channels : (k + 1) * channels, :]

    def part(early, late, begin):
        ref, at = (early, begin) if begin < SPAN else (late, begin - SPAN)
        return ref[at : at + STEP, :]

    for begin in range(0, rows, STEP):
        here = slice(begin, begin + STEP)
        hidden = dot(part(mixed_early, mixed_late, begin), out_weight[...]) + out_bias[...]
        output[here, :] = (signal[here, :].astype(F32) + hidden).astype(BF16)
        total = cot[here, :].astype(F32)
        for k in range(TAPS):
            if begin + k * STEP < rows:
                total = total + dot_columns(part(dpre_early, dpre_late, begin + k * STEP), tap(k))
        partial[here, :] = total


def join_kernel(last, partial, incoming, out):
    rows = partial.shape[0]
    out[: rows - SPAN, :] = partial[: rows - SPAN, :].astype(BF16)
    more = jnp.where(last[0] == 1, jnp.zeros(incoming.shape, F32), incoming[...].astype(F32))
    out[rows - SPAN :, :] = (partial[rows - SPAN :, :] + more).astype(BF16)


def piece_height(rows, pieces):
    return -(-rows // (pieces * 16)) * 16


def widened(block):
    wide = block.astype(F32)
    return wide[:SUBLANES] + wide[SUBLANES:]


def narrowed(total):
    high = total.astype(BF16).astype(F32)
    return jnp.concatenate([high, total - high], 0).astype(BF16)


def split_kernel(radix, more, *refs):
    digit, main, bias, received = refs[0], refs[1], refs[2], refs[3 : 3 + more]
    sends, keep = refs[3 + more : -1], refs[-1]
    rows, end = sends[0].shape[0] - BIAS_ROWS, main.shape[0]
    total = bias[...]
    for ref in received:
        total = total + widened(ref[end:, :])
    for k in range(radix):
        start = pl.multiple_of((digit[0] ^ k) * rows, 16)
        block = main[pl.ds(start, rows), :]
        for ref in received:
            block = block + ref[pl.ds(start, rows), :].astype(F32)
        if k:
            sends[k - 1][:rows, :] = block.astype(BF16)
            sends[k - 1][rows:, :] = narrowed(total)
        else:
            keep[:rows, :] = block
            keep[rows:, :] = total


def finish_kernel(scale, *refs):
    keep, received, out = refs[0], refs[1:-1], refs[-1]
    rows = out.shape[0] - BIAS_ROWS
    block, total = keep[:rows, :], keep[rows:, :]
    for ref in received:
        block = block + ref[:rows, :].astype(F32)
        total = total + widened(ref[rows:, :])
    out[:rows, :] = (block * scale).astype(BF16)
    out[rows:, :] = narrowed(total * scale)


def place_kernel(radix, taker, scalars, given, *refs):
    parts, out = refs[:radix], refs[radix]
    rows = parts[0].shape[0] - BIAS_ROWS
    own = jnp.where(scalars[1] == taker, given[...], parts[0][...])
    for k in range(radix):
        block = parts[k][...] if k else own
        index = scalars[0] ^ k
        out[pl.ds(pl.multiple_of(index * rows, 16), rows), :] = block[:rows]

        @pl.when(index == 0)
        def _():
            out[radix * rows :, :] = block[rows:]


def spread_kernel(radix, taker, pieces, scalars, given, *refs):
    parts, forwarded = refs[:radix], refs[radix : 2 * radix - 1]
    conv, proj, biases, whole = refs[2 * radix - 1 :]
    rows = parts[0].shape[0] - BIAS_ROWS
    for k in range(radix):
        other = forwarded[k - 1] if k else given
        block = jnp.where((scalars[1] == taker) == (k > 0), parts[k][...], other[...])
        index = scalars[0] ^ k
        whole[pl.ds(pl.multiple_of(index * rows, 16), rows), :] = block[:rows]

        @pl.when(index == 0)
        def _():
            biases[...] = widened(block[rows:])

    at = 0
    for piece in range(pieces):
        for out in (conv, proj):
            height = piece_height(out.shape[0], pieces)
            begin = piece * height
            count = min(height, out.shape[0] - begin)
            for column in range(0, out.shape[1], LANES):
                if count > 0:
                    out[begin : begin + count, column : column + LANES] = whole[
                        at : at + count, :
                    ].astype(F32)
                at += height


def digits_of(count):
    digits = []
    while count > 1:
        digits.append(4 if count % 4 == 0 else 2)
        count //= digits[-1]
    return digits


def place_of():
    runs = lax.axis_size("run")
    chips = lax.axis_size("tm") * runs // 2
    flat = lax.axis_index("tm") * runs + lax.axis_index("run")
    return chips, flat // 2, flat % 2


def swapped(array):
    chips = place_of()[0]
    return lax.ppermute(array, BOTH, [(i, i ^ 1) for i in range(2 * chips)])


def crossed(array, source, step):
    chips = place_of()[0]
    pairs = [(2 * c + source, 2 * (c ^ step) + 1 - source) for c in range(chips)]
    pairs += [(2 * c + 1 - source, 2 * c + source) for c in range(chips)]
    return lax.ppermute(array, BOTH, pairs)


def summed_everywhere(main, bias, message, scale, shapes):
    chips, chip, core = place_of()
    digits = digits_of(chips)
    received = [swapped(message)]
    weight, source, levels = 1, 0, []
    for level, radix in enumerate(digits):
        digit = (chip // weight) % radix
        rows = main.shape[0] // radix
        *sends, keep = call(
            functools.partial(split_kernel, radix, len(received)),
            [shape(BF16, rows + BIAS_ROWS, LANES)] * (radix - 1) + [shape(F32, rows + SUBLANES, LANES)],
            (digit.reshape(1), main, bias, *received),
            1,
        )
        if level:
            keep = swapped(keep)
        received = [crossed(sends[k - 1], source, k * weight) for k in range(1, radix)]
        main, bias = keep[:rows], keep[rows:]
        levels.append((radix, weight, digit, source))
        weight *= radix
        source = 1 - source
    (part,) = call(
        functools.partial(finish_kernel, scale),
        [shape(BF16, rows + BIAS_ROWS, LANES)],
        (keep, *received),
    )
    for level in reversed(range(len(levels))):
        radix, weight, digit, _ = levels[level]
        given = swapped(part)
        parts = [part] + [crossed(part, source, k * weight) for k in range(1, radix)]
        scalars = jnp.stack([digit, core])
        if level:
            rows = part.shape[0] - BIAS_ROWS
            (part,) = call(
                functools.partial(place_kernel, radix, 1 - source),
                [shape(BF16, radix * rows + BIAS_ROWS, LANES)],
                (scalars, given, *parts),
                1,
            )
            source = 1 - source
    forwarded = [swapped(p) for p in parts[1:]]
    return call(
        functools.partial(spread_kernel, radix, 1 - source, chips),
        list(shapes) + [shape(F32, SUBLANES, LANES)],
        (scalars, given, *parts, *forwarded),
        1,
        scratch=[pltpu.VMEM((main_rows(shapes, chips), LANES), BF16)],
    )


def main_rows(shapes, pieces):
    return pieces * sum(piece_height(s.shape[0], pieces) * s.shape[1] // LANES for s in shapes)


def local(signal, conv_weight, conv_bias, out_weight, out_bias, cotangent):
    rows, channels = signal.shape[1:]
    wide = 2 * channels
    size = lax.axis_size("tm")
    index = lax.axis_index("tm")
    x, cot = signal[0], cotangent[0]
    history = lax.ppermute(x[rows - SPAN :], "tm", [(i, (i + 1) % size) for i in range(size)])
    late = rows - SPAN
    preact, dmixed, mixed_late, dpre_late, conv, proj, bias = call(
        late_kernel,
        [
            shape(F32, SPAN, wide), shape(F32, SPAN, channels), shape(BF16, late, channels),
            shape(BF16, late, wide), shape(F32, TAPS * channels, wide), shape(F32, channels, channels),
            shape(F32, SUBLANES, wide + channels),
        ],
        (x, conv_weight, conv_bias.reshape(1, -1), out_weight, cot),
        flops=3 * rows * channels * channels * 8,
    )
    chips = place_of()[0]
    shapes = [shape(F32, TAPS * channels, wide), shape(F32, channels, channels)]
    total = main_rows(shapes, chips)
    mixed_early, dpre_early, main, bias, message = call(
        functools.partial(early_kernel, total // chips),
        [
            shape(BF16, SPAN, channels), shape(BF16, SPAN, wide), shape(F32, total, LANES),
            shape(F32, SUBLANES, LANES), shape(BF16, total + BIAS_ROWS, LANES),
        ],
        (
            (index == 0).astype(jnp.int32).reshape(1), history, x, conv_weight, cot,
            preact, dmixed, conv, proj, bias,
        ),
        1,
        flops=2 * rows * channels * channels * 8,
        scratch=[pltpu.VMEM((SPAN, channels), BF16)] + [pltpu.VMEM(s.shape, F32) for s in shapes],
    )
    (back,) = call(back_kernel, [shape(BF16, SPAN, channels)], (dpre_early, conv_weight))
    output, partial = call(
        own_kernel,
        [shape(BF16, rows, channels), shape(F32, rows, channels)],
        (
            x, conv_weight, out_weight, out_bias.reshape(1, -1), cot,
            mixed_early, mixed_late, dpre_early, dpre_late,
        ),
        flops=2 * rows * channels * channels * 8,
    )
    incoming = lax.ppermute(back, "tm", [((i + 1) % size, i) for i in range(size)])
    (grad_signal,) = call(
        join_kernel,
        [shape(BF16, rows, channels)],
        ((index == size - 1).astype(jnp.int32).reshape(1), partial, incoming),
        1,
    )
    scale = float(signal.shape[0] * lax.axis_size("run") * rows * size) ** -0.5
    grad_conv, grad_proj, biases = summed_everywhere(main, bias, message, scale, shapes)
    biases = biases.reshape(-1)
    return (
        output[None],
        grad_signal[None],
        grad_conv,
        biases[:wide],
        grad_proj,
        biases[wide : wide + channels],
    )


def solution(mesh):
    placed = (P("run", "tm", None), P(), P(), P(), P(), P("run", "tm", None))
    return jax.shard_map(
        local,
        mesh=mesh,
        in_specs=placed,
        out_specs=(P("run", "tm", None), P("run", "tm", None), P(), P(), P(), P()),
        check_vma=False,
    )
```

```python
import functools

import jax
import jax.numpy as jnp
from jax import lax
from jax.experimental import pallas as pl
from jax.experimental.pallas import tpu as pltpu
from jax.sharding import PartitionSpec as P

STEP = 256
TAPS = 3
SPAN = (TAPS - 1) * STEP
BOTH = ("tm", "run")
LANES = 128
SUBLANES = 8
BIAS_ROWS = 2 * SUBLANES
F32 = jnp.float32
BF16 = jnp.bfloat16
VMEM = pl.BlockSpec(memory_space=pltpu.VMEM)
ANY = pl.BlockSpec(memory_space=pl.ANY)
HBM = pl.BlockSpec(memory_space=pltpu.HBM)
MIB = 1024 * 1024


def call(kernel, out_shape, args, flops=0, scratch=(), after=(), far=(), alias=None):
    moved = sum(a.size * a.dtype.itemsize for a in args)
    inner = kernel
    if after:
        count = len(args)
        inner = lambda *refs: kernel(*refs[:count], *refs[count + len(after) :])
    ins = [HBM if i in far else VMEM for i in range(len(args))]
    outs = [HBM if -1 - i in far else VMEM for i in range(len(out_shape))]
    placed = [
        pltpu.with_memory_space_constraint(a, pltpu.HBM if i in far else pltpu.VMEM)
        for i, a in enumerate(args)
    ]
    return pl.pallas_call(
        inner,
        out_shape=out_shape,
        in_specs=ins + [ANY] * len(after),
        out_specs=outs,
        scratch_shapes=list(scratch),
        input_output_aliases=alias or {},
        cost_estimate=pl.CostEstimate(flops=0, bytes_accessed=8, transcendentals=0),
        compiler_params=pltpu.CompilerParams(vmem_limit_bytes=(8 if count_of_chips() <= 16 else 40) * MIB),
    )(*placed, *after)


def held(dtype, *dims):
    return pltpu.VMEM(dims, dtype)


def shape(dtype, *dims):
    return jax.ShapeDtypeStruct(dims, dtype)


def count_of_chips():
    return lax.axis_size("tm") * lax.axis_size("run") // 2


def place_of():
    flat = lax.axis_index("tm") * lax.axis_size("run") + lax.axis_index("run")
    return flat // 2, lax.rem(flat, 2)


def digit_of(level):
    chip = place_of()[0]
    return sum(lax.rem(chip // (1 << bit), 2) * (1 << i) for i, bit in enumerate(level))


def steps_of(level):
    last = (1 << len(level)) - 1
    return [last, *range(1, last)]


def step_between(level, k):
    return sum(1 << bit for i, bit in enumerate(level) if k >> i & 1)


TOKEN = held(F32, SUBLANES, LANES)


def dot(a, b):
    return jnp.dot(a, b, preferred_element_type=F32)


def dot_rows(a, b):
    return lax.dot_general(a, b, (((0,), (0,)), ((), ())), preferred_element_type=F32)


def dot_columns(a, b):
    return lax.dot_general(a, b, (((1,), (1,)), ((), ())), preferred_element_type=F32)


def gates(preact, dmixed):
    channels = dmixed.shape[1]
    filtered = jnp.tanh(preact[:, :channels])
    gated = jax.nn.sigmoid(preact[:, channels:])
    mixed = filtered * gated
    dfiltered = dmixed * gated * (1.0 - filtered * filtered)
    dgated = dmixed * mixed * (1.0 - gated)
    return mixed.astype(BF16), dfiltered.astype(BF16), dgated.astype(BF16)


def late_kernel(
    signal_in, weight_in, bias, out_weight_in, cot_in,
    signal, weight, out_weight, cot,
    preact_out, dmixed_out, mixed_out, dpre_out, grad_conv, grad_proj, grad_bias, sems,
):
    rows, channels = signal.shape
    pairs = ((signal_in, signal), (weight_in, weight), (cot_in, cot), (out_weight_in, out_weight))
    copies = [pltpu.make_async_copy(a, b, sems.at[i]) for i, (a, b) in enumerate(pairs)]
    for copy in copies:
        copy.start()
    tap = lambda k: weight[k * channels : (k + 1) * channels, :]
    copies[0].wait()
    copies[1].wait()
    preact_out[...] = dot(signal[:SPAN, :], tap(0)) + bias[...]
    for k in range(1, TAPS - 1):
        preact_out[k * STEP :, :] += dot(signal[: SPAN - k * STEP, :], tap(k))
    copies[2].wait()
    copies[3].wait()
    dmixed_out[...] = dot_columns(cot[:SPAN, :], out_weight[...])
    for begin in range(SPAN, rows, STEP):
        here = slice(begin, begin + STEP)
        at = slice(begin - SPAN, begin - SPAN + STEP)
        preact = bias[...]
        for k in range(TAPS):
            preact = preact + dot(signal[begin - k * STEP : begin - k * STEP + STEP, :], tap(k))
        mixed, dfiltered, dgated = gates(preact, dot_columns(cot[here, :], out_weight[...]))
        mixed_out[at, :] = mixed
        dpre_out[at, :channels] = dfiltered
        dpre_out[at, channels:] = dgated
    dpre = dpre_out[...]
    for k in range(TAPS):
        grad_conv[k * channels : (k + 1) * channels, :] = dot_rows(
            signal[SPAN - k * STEP : rows - k * STEP, :], dpre
        )
    grad_proj[...] = dot_rows(mixed_out[...], cot[SPAN:, :])
    ones = jnp.ones((BIAS_ROWS, rows), BF16)
    grad_bias[:, : 2 * channels] = dot(ones[:, : rows - SPAN], dpre)[:SUBLANES]
    grad_bias[:, 2 * channels :] = dot(ones, cot[...])[:SUBLANES]


def early_kernel(
    level, pieces, history, signal, weight, cot, preact_in, dmixed_in, conv_in, proj_in, bias_in,
    mixed_out, dpre_out, *refs,
):
    radix, digit, core = 1 << len(level), digit_of(level), place_of()[1]
    turn = steps_of(level)
    first = lax.axis_index("tm") == 0
    own, offered = refs[:radix], refs[radix : 2 * radix - 1]
    past, grad_conv, grad_proj = refs[2 * radix - 1 :]
    rows, channels = signal.shape
    tap = lambda k: weight[k * channels : (k + 1) * channels, :]
    past[...] = jnp.where(first, jnp.zeros_like(history), history[...])
    for begin in range(0, SPAN, STEP):
        here = slice(begin, begin + STEP)
        preact = preact_in[here, :]
        for k in range(begin // STEP + 1, TAPS):
            source = SPAN + begin - k * STEP
            preact = preact + dot(past[source : source + STEP, :], tap(k))
        mixed, dfiltered, dgated = gates(preact, dmixed_in[here, :])
        mixed_out[here, :] = mixed
        dpre_out[here, :channels] = dfiltered
        dpre_out[here, channels:] = dgated
    dpre = dpre_out[...]
    for k in range(TAPS):
        at = slice(k * channels, (k + 1) * channels)
        total = conv_in[at, :]
        if k:
            total = total + dot_rows(past[SPAN - k * STEP :, :], dpre[: k * STEP, :])
        if k < TAPS - 1:
            total = total + dot_rows(signal[: SPAN - k * STEP, :], dpre[k * STEP :, :])
        grad_conv[at, :] = total
    grad_proj[: proj_in.shape[0], :] = proj_in[...] + dot_rows(mixed_out[...], cot[:SPAN, :])
    for grad, filled in ((grad_conv, conv_in.shape[0]), (grad_proj, proj_in.shape[0])):
        if filled < grad.shape[0]:
            grad[filled:, :] = jnp.zeros((grad.shape[0] - filled, grad.shape[1]), F32)
    ones = jnp.ones((BIAS_ROWS, SPAN), BF16)
    columns = dot(ones, dpre)[:SUBLANES]
    bias = bias_in[...]
    bias = jnp.concatenate([bias[:, : 2 * channels] + columns, bias[:, 2 * channels :]], 1)
    lines = [bias[:1, c : c + LANES] for c in range(0, bias.shape[1], LANES)]
    lines += [jnp.zeros((1, LANES), F32)] * (SUBLANES - len(lines))
    bias = jnp.concatenate(lines, 0)
    for k in range(radix):
        at = 0
        for piece in range(pieces // radix):
            index = (digit ^ k) * (pieces // radix) + piece
            for grad in (grad_conv, grad_proj):
                height = grad.shape[0] // pieces
                begin = pl.multiple_of(index * height, 16)
                for column in range(0, grad.shape[1], LANES):
                    block = grad[pl.ds(begin, height), column : column + LANES]
                    own[k][at : at + height, :] = block
                    if k in turn[1:]:
                        offered[turn.index(k)][at : at + height, :] = block.astype(BF16)
                    at += height
        own[k][at:, :] = bias
        if k in turn[1:]:
            offered[turn.index(k)][at:, :] = narrowed(bias)
    offered[0][at:, :] = narrowed(bias)
    for mine, k in ((0, 0), (1, turn[0])):

        @pl.when(core == mine)
        def _():
            offered[0][:at, :] = own[k][:at, :].astype(BF16)


def back_kernel(dpre, weight, out):
    channels = out.shape[1]
    tap = lambda k: weight[k * channels : (k + 1) * channels, :]
    for begin in range(0, SPAN, STEP):
        total = dot_columns(dpre[begin : begin + STEP, :], tap(TAPS - 1))
        for k in range(1, TAPS - 1):
            source = begin - SPAN + k * STEP
            if source >= 0:
                total = total + dot_columns(dpre[source : source + STEP, :], tap(k))
        out[begin : begin + STEP, :] = total.astype(BF16)


def own_kernel(signal, weight, out_weight, out_bias, cot, mixed_early, mixed_late, dpre_early, dpre_late, output, partial, token):
    rows, channels = signal.shape
    tap = lambda k: weight[k * channels : (k + 1) * channels, :]
    token[...] = jnp.zeros_like(token)

    def part(early, late, begin):
        ref, at = (early, begin) if begin < SPAN else (late, begin - SPAN)
        return ref[at : at + STEP, :]

    for begin in range(0, rows, STEP):
        here = slice(begin, begin + STEP)
        hidden = dot(part(mixed_early, mixed_late, begin), out_weight[...]) + out_bias[...]
        output[here, :] = (signal[here, :].astype(F32) + hidden).astype(BF16)
        total = cot[here, :].astype(F32)
        for k in range(TAPS):
            if begin + k * STEP < rows:
                total = total + dot_columns(part(dpre_early, dpre_late, begin + k * STEP), tap(k))
        partial[here, :] = total


PLANE = 4


def relay_pairs():
    runs, size = lax.axis_size("run"), lax.axis_size("tm")
    pairs = []
    for t in range(size):
        for r in range(runs):
            to = ((t - PLANE) % size) * runs + r if t % PLANE == 0 else t * runs + (r ^ 1)
            pairs.append((t * runs + r, to))
    return pairs


def plane_pairs():
    size = lax.axis_size("tm")
    return [(t, t - 1 if t % PLANE else t + PLANE - 1) for t in range(size)]


def relay_kernel(back, relayed, onward):
    first = lax.rem(lax.axis_index("tm"), PLANE) == 0
    onward[...] = jnp.where(first, relayed[...], back[...])


def join_kernel(partial, incoming, out, token):
    token[...] = jnp.zeros_like(token)
    rows = partial.shape[0]
    last = lax.axis_index("tm") == lax.axis_size("tm") - 1
    out[: rows - SPAN, :] = partial[: rows - SPAN, :].astype(BF16)
    more = jnp.where(last, jnp.zeros(incoming.shape, F32), incoming[...].astype(F32))
    out[rows - SPAN :, :] = (partial[rows - SPAN :, :] + more).astype(BF16)


def piece_height(rows, pieces):
    return -(-rows // (pieces * 16)) * 16


def widened(block):
    wide = block.astype(F32)
    return wide[:SUBLANES] + wide[SUBLANES:]


def narrowed(total):
    high = total.astype(BF16).astype(F32)
    return jnp.concatenate([high, total - high], 0).astype(BF16)


def first_kernel(keep_own, send_own, received, keep, send):
    end = send.shape[0] - BIAS_ROWS
    more, bias = received[:end, :].astype(F32), widened(received[end:, :])
    keep[:end, :] = keep_own[:end, :] + more
    keep[end:, :] = keep_own[end:, :] + bias
    send[:end, :] = (send_own[:end, :] + more).astype(BF16)
    send[end:, :] = narrowed(send_own[end:, :] + bias)


def next_kernel(send_own, received, send):
    end = send.shape[0] - BIAS_ROWS
    send[:end, :] = (send_own[:end, :] + received[:end, :].astype(F32)).astype(BF16)
    send[end:, :] = narrowed(send_own[end:, :] + widened(received[end:, :]))


def split_kernel(level, more, *refs):
    radix, digit = 1 << len(level), digit_of(level)
    main, received = refs[0], refs[1 : 1 + more]
    sends, keep = refs[1 + more : -1], refs[-1]
    rows, end = sends[0].shape[0] - BIAS_ROWS, main.shape[0] - SUBLANES
    total = main[end:, :]
    for ref in received:
        total = total + widened(ref[end:, :])
    for k in range(radix):
        start = pl.multiple_of((digit ^ k) * rows, 16)
        block = main[pl.ds(start, rows), :]
        for ref in received:
            block = block + ref[pl.ds(start, rows), :].astype(F32)
        if k:
            sends[k - 1][:rows, :] = block.astype(BF16)
            sends[k - 1][rows:, :] = narrowed(total)
        else:
            keep[:rows, :] = block
            keep[rows:, :] = total


def finish_kernel(scale, *refs):
    keep, received, out = refs[0], refs[1:-1], refs[-1]
    rows = out.shape[0] - BIAS_ROWS
    block, total = keep[:rows, :], keep[rows:, :]
    for ref in received:
        block = block + ref[:rows, :].astype(F32)
        total = total + widened(ref[rows:, :])
    out[:rows, :] = (block * scale).astype(BF16)
    out[rows:, :] = narrowed(total * scale)


def place_kernel(level, taker, given, *refs):
    radix, digit, core = 1 << len(level), digit_of(level), place_of()[1]
    parts, out = refs[:radix], refs[radix]
    rows = parts[0].shape[0] - BIAS_ROWS
    own = jnp.where(core == taker, given[...], parts[0][...])
    for k in range(radix):
        block = parts[k][...] if k else own
        index = digit ^ k
        out[pl.ds(pl.multiple_of(index * rows, 16), rows), :] = block[:rows]

        @pl.when(index == 0)
        def _():
            out[radix * rows :, :] = block[rows:]


def spread_kernel(steps, level, taker, pieces, *refs):
    count = len(steps)
    ends = steps[-1] != 0 and count == 1
    digit, core = digit_of(level), place_of()[1]
    direct, passed, refs = refs[:count], refs[count : 2 * count], refs[2 * count :]
    before, refs = (refs[0], refs[3:]) if ends else (None, refs)
    (conv, proj), refs = refs[:2], refs[2:]
    bias_out, (wide_conv, wide_proj, wide_bias, sems) = refs[:-4], refs[-4:]
    bias = before[...] if ends else jnp.zeros((SUBLANES, LANES), F32)
    copies = []

    def send(source, target, *at):
        copies.append(pltpu.make_async_copy(source, target, sems.at[at]))
        copies[-1].start()

    for k, here, there in zip(steps, direct, passed):
        end = here.shape[0] - BIAS_ROWS
        block = jnp.where((core == taker) == (k > 0), here[end:, :], there[end:, :])
        bias = jnp.where((digit ^ k) == 0, widened(block), bias)
    if ends:
        wide_bias[...] = jnp.concatenate([bias[i : i + 1, :] for i in range(SUBLANES)], 1)
        column = 0
        for n, out in enumerate(bias_out):
            send(wide_bias.at[:, column : column + out.shape[1]], out, count, n)
            column += out.shape[1]
    else:
        bias_out[0][...] = bias
    for n, (k, here, there) in enumerate(zip(steps, direct, passed)):
        block = jnp.where((core == taker) == (k > 0), here[...], there[...])
        at = 0
        for piece in range(pieces):
            for wide in (wide_conv, wide_proj):
                height = wide.shape[1] // pieces
                for column in range(0, wide.shape[2], LANES):
                    wide[n, piece * height : (piece + 1) * height, column : column + LANES] = (
                        block[at : at + height].astype(F32)
                    )
                    at += height
        for m, (wide, out) in enumerate(((wide_conv, conv), (wide_proj, proj))):
            height = wide.shape[1]
            start = pl.multiple_of((digit ^ k) * height, 16)
            send(wide.at[n], out.at[pl.ds(start, height), :], n, m)
    for copy in copies:
        copy.wait()


def levels_of(chips):
    count = chips.bit_length() - 1
    bits = list(range(count))
    return [tuple(bits[i : i + 2]) for i in range(0, count, 2)]


def swapped(array):
    chips = count_of_chips()
    return lax.ppermute(array, BOTH, [(i, i ^ 1) for i in range(2 * chips)])


def crossed(array, source, step):
    chips = count_of_chips()
    pairs = [(2 * c + source, 2 * (c ^ step) + 1 - source) for c in range(chips)]
    pairs += [(2 * c + 1 - source, 2 * c + source) for c in range(chips)]
    return lax.ppermute(array, BOTH, pairs)


def summed_everywhere(own, offered, scale, heights, widths, fill):
    chips = count_of_chips()
    levels = levels_of(chips)
    radix, turn = 1 << len(levels[0]), steps_of(levels[0])
    rows = own[0].shape[0] - SUBLANES
    exchanged = [swapped(message) for message in offered]
    keep, send = call(
        first_kernel,
        [held(F32, rows + SUBLANES, LANES), held(BF16, rows + BIAS_ROWS, LANES)],
        (own[0], own[turn[0]], exchanged[0]),
        after=fill(0, ()),
    )
    received = [crossed(send, 0, step_between(levels[0], turn[0]))]
    for k, message in zip(turn[1:], exchanged[1:]):
        (send,) = call(next_kernel, [held(BF16, rows + BIAS_ROWS, LANES)], (own[k], message))
        received.append(crossed(send, 0, step_between(levels[0], k)))
    ready = fill(1, (send,))
    source = 1
    for level in range(1, len(levels)):
        radix = 1 << len(levels[level])
        rows //= radix
        *sends, keep = call(
            functools.partial(split_kernel, levels[level], len(received)),
            [held(BF16, rows + BIAS_ROWS, LANES)] * (radix - 1) + [held(F32, rows + SUBLANES, LANES)],
            (keep, *received),
            after=ready if level == 1 else (),
        )
        if level == 1:
            fill(2, (sends[0],))
        keep = swapped(keep)
        received = [
            crossed(sends[k - 1], source, step_between(levels[level], k))
            for k in steps_of(levels[level])
        ]
        source = 1 - source
    (part,) = call(
        functools.partial(finish_kernel, scale),
        [held(BF16, rows + BIAS_ROWS, LANES)],
        (keep, *received),
        after=ready if len(levels) == 1 else (),
    )
    if len(levels) == 1:
        fill(2, (part,))
    for level in reversed(range(len(levels))):
        radix = 1 << len(levels[level])
        crossing = {
            k: crossed(part, source, step_between(levels[level], k)) for k in steps_of(levels[level])
        }
        given = swapped(part)
        parts = [part] + [crossing[k] for k in range(1, radix)]
        if level:
            rows = part.shape[0] - BIAS_ROWS
            (part,) = call(
                functools.partial(place_kernel, levels[level], 1 - source),
                [held(BF16, radix * rows + BIAS_ROWS, LANES)],
                (given, *parts),
                after=fill(3, ()) if level == 1 else (),
            )
            source = 1 - source
    taker, pieces = 1 - source, chips // radix
    whole = [shape(F32, chips * h, w) for h, w in zip(heights, widths)]

    def room(count):
        return [
            *[pltpu.VMEM((count, pieces * h, w), F32) for h, w in zip(heights, widths)],
            pltpu.VMEM((1, SUBLANES * LANES), F32),
            pltpu.SemaphoreType.DMA((count + 1, 2)),
        ]

    early, last = [0, *turn[:-1]], turn[-1]
    forwarded = [given] + [swapped(parts[k]) for k in early[1:]]
    conv, proj, bias = call(
        functools.partial(spread_kernel, early, levels[0], taker, pieces),
        whole + [held(F32, SUBLANES, LANES)],
        (*[parts[k] for k in early], *forwarded),
        scratch=room(len(early)),
        far=(-1, -2),
    )
    return call(
        functools.partial(spread_kernel, [last], levels[0], taker, pieces),
        whole + [shape(F32, 1, w) for w in widths],
        (parts[last], swapped(parts[last]), bias, conv, proj),
        scratch=room(1),
        far=(-1, -2, -3, -4, 3, 4),
        alias={3: 0, 4: 1},
    )


def local(signal, conv_weight, conv_bias, out_weight, out_bias, cotangent):
    rows, channels = signal.shape[1:]
    wide = 2 * channels
    late = rows - SPAN
    size = lax.axis_size("tm")
    chips = count_of_chips()
    level = levels_of(chips)[0]
    radix = 1 << len(level)
    widths = (wide, channels)
    heights = [piece_height(n, chips) for n in (TAPS * channels, channels)]
    piece = chips // radix * sum(h * w // LANES for h, w in zip(heights, widths))

    history = lax.ppermute(signal[0, late:], "tm", [(i, (i + 1) % size) for i in range(size)])
    x, weight, proj_weight, cot, preact, dmixed, mixed_late, dpre_late, conv, proj, bias = call(
        late_kernel,
        [
            held(BF16, rows, channels), held(BF16, TAPS * channels, wide), held(BF16, channels, channels),
            held(BF16, rows, channels),
            held(F32, SPAN, wide), held(F32, SPAN, channels), held(BF16, late, channels),
            held(BF16, late, wide), held(F32, TAPS * channels, wide), held(F32, channels, channels),
            held(F32, SUBLANES, wide + channels),
        ],
        (signal[0], conv_weight, conv_bias.reshape(1, -1), out_weight, cotangent[0]),
        flops=3 * rows * channels * channels * 8,
        scratch=[pltpu.SemaphoreType.DMA((4,))],
        far=(0, 1, 3, 4),
    )
    mixed_early, dpre_early, *pieces = call(
        functools.partial(early_kernel, level, chips),
        [held(BF16, SPAN, channels), held(BF16, SPAN, wide)]
        + [held(F32, piece + SUBLANES, LANES)] * radix
        + [held(BF16, piece + BIAS_ROWS, LANES)] * (radix - 1),
        (
            history, x, weight, cot, preact, dmixed, conv, proj, bias,
        ),
        flops=2 * rows * channels * channels * 8,
        scratch=[pltpu.VMEM((SPAN, channels), BF16)]
        + [pltpu.VMEM((chips * h, w), F32) for h, w in zip(heights, widths)],
    )
    results = {}

    def fill(stage, after):
        if stage == 0:
            (results["back"],) = call(
                back_kernel, [held(BF16, SPAN, channels)], (dpre_early, weight), after=after
            )
            results["relayed"] = lax.ppermute(results["back"], BOTH, relay_pairs())
            return (results["back"],)
        if stage == 1:
            results["output"], results["partial"], token = call(
                own_kernel,
                [shape(BF16, rows, channels), held(F32, rows, channels), TOKEN],
                (
                    x, weight, proj_weight, out_bias.reshape(1, -1), cot,
                    mixed_early, mixed_late, dpre_early, dpre_late,
                ),
                after=after,
            )
            return (token,)
        if stage == 2:
            (onward,) = call(
                relay_kernel,
                [held(BF16, SPAN, channels)],
                (results["back"], results["relayed"]),
                after=after,
            )
            results["incoming"] = lax.ppermute(onward, "tm", plane_pairs())
            return ()
        results["grad_signal"], token = call(
            join_kernel,
            [shape(BF16, rows, channels), TOKEN],
            (
                results["partial"],
                results["incoming"],
            ),
            after=after,
        )
        return (token,)

    scale = float(signal.shape[0] * lax.axis_size("run") * rows * size) ** -0.5
    grad_conv, grad_proj, grad_cbias, grad_pbias = summed_everywhere(
        pieces[:radix], pieces[radix:], scale, heights, widths, fill
    )
    return (
        results["output"][None],
        results["grad_signal"][None],
        grad_conv[: TAPS * channels],
        grad_cbias[0],
        grad_proj[:channels],
        grad_pbias[0],
    )


def solution(mesh):
    placed = (P("run", "tm", None), P(), P(), P(), P(), P("run", "tm", None))
    return jax.shard_map(
        local,
        mesh=mesh,
        in_specs=placed,
        out_specs=(P("run", "tm", None), P("run", "tm", None), P(), P(), P(), P()),
        check_vma=False,
    )
```

```python
import functools

import jax
import jax.numpy as jnp
from jax import lax
from jax.experimental import pallas as pl
from jax.experimental.pallas import tpu as pltpu
from jax.sharding import PartitionSpec as P

STEP = 256
TAPS = 3
SPAN = (TAPS - 1) * STEP
BOTH = ("tm", "run")
LANES = 128
SUBLANES = 8
BIAS_ROWS = 2 * SUBLANES
F32 = jnp.float32
BF16 = jnp.bfloat16
VMEM = pl.BlockSpec(memory_space=pltpu.VMEM)
ANY = pl.BlockSpec(memory_space=pl.ANY)
HBM = pl.BlockSpec(memory_space=pltpu.HBM)
MIB = 1024 * 1024


def call(kernel, out_shape, args, flops=0, scratch=(), after=(), far=(), alias=None):
    moved = sum(a.size * a.dtype.itemsize for a in args)
    inner = kernel
    if after:
        count = len(args)
        inner = lambda *refs: kernel(*refs[:count], *refs[count + len(after) :])
    ins = [HBM if i in far else VMEM for i in range(len(args))]
    outs = [HBM if -1 - i in far else VMEM for i in range(len(out_shape))]
    placed = [
        pltpu.with_memory_space_constraint(a, pltpu.HBM if i in far else pltpu.VMEM)
        for i, a in enumerate(args)
    ]
    return pl.pallas_call(
        inner,
        out_shape=out_shape,
        in_specs=ins + [ANY] * len(after),
        out_specs=outs,
        scratch_shapes=list(scratch),
        input_output_aliases=alias or {},
        cost_estimate=pl.CostEstimate(flops=flops, bytes_accessed=8, transcendentals=0),
        compiler_params=pltpu.CompilerParams(vmem_limit_bytes=(8 if count_of_chips() <= 16 else 40) * MIB),
    )(*placed, *after)


def held(dtype, *dims):
    return pltpu.VMEM(dims, dtype)


def shape(dtype, *dims):
    return jax.ShapeDtypeStruct(dims, dtype)


def count_of_chips():
    return lax.axis_size("tm") * lax.axis_size("run") // 2


def place_of():
    flat = lax.axis_index("tm") * lax.axis_size("run") + lax.axis_index("run")
    return flat // 2, lax.rem(flat, 2)


def digit_of(level):
    chip = place_of()[0]
    return sum(lax.rem(chip // (1 << bit), 2) * (1 << i) for i, bit in enumerate(level))


def steps_of(level):
    last = (1 << len(level)) - 1
    return [last, *range(1, last)]


def step_between(level, k):
    return sum(1 << bit for i, bit in enumerate(level) if k >> i & 1)


TOKEN = held(F32, SUBLANES, LANES)


def dot(a, b):
    return jnp.dot(a, b, preferred_element_type=F32)


def dot_rows(a, b):
    return lax.dot_general(a, b, (((0,), (0,)), ((), ())), preferred_element_type=F32)


def dot_columns(a, b):
    return lax.dot_general(a, b, (((1,), (1,)), ((), ())), preferred_element_type=F32)


def gates(preact, dmixed):
    channels = dmixed.shape[1]
    filtered = jnp.tanh(preact[:, :channels])
    gated = jax.nn.sigmoid(preact[:, channels:])
    mixed = filtered * gated
    dfiltered = dmixed * gated * (1.0 - filtered * filtered)
    dgated = dmixed * mixed * (1.0 - gated)
    return mixed.astype(BF16), dfiltered.astype(BF16), dgated.astype(BF16)


def late_kernel(
    signal_in, weight_in, bias, out_weight_in, cot_in,
    signal, weight, out_weight, cot,
    preact_out, dmixed_out, mixed_out, dpre_out, grad_conv, grad_proj, grad_bias, sems,
):
    rows, channels = signal.shape
    pairs = ((signal_in, signal), (weight_in, weight), (cot_in, cot), (out_weight_in, out_weight))
    copies = [pltpu.make_async_copy(a, b, sems.at[i]) for i, (a, b) in enumerate(pairs)]
    for copy in copies:
        copy.start()
    tap = lambda k: weight[k * channels : (k + 1) * channels, :]
    copies[0].wait()
    copies[1].wait()
    preact_out[...] = dot(signal[:SPAN, :], tap(0)) + bias[...]
    for k in range(1, TAPS - 1):
        preact_out[k * STEP :, :] += dot(signal[: SPAN - k * STEP, :], tap(k))
    copies[2].wait()
    copies[3].wait()
    dmixed_out[...] = dot_columns(cot[:SPAN, :], out_weight[...])
    for begin in range(SPAN, rows, STEP):
        here = slice(begin, begin + STEP)
        at = slice(begin - SPAN, begin - SPAN + STEP)
        preact = bias[...]
        for k in range(TAPS):
            preact = preact + dot(signal[begin - k * STEP : begin - k * STEP + STEP, :], tap(k))
        mixed, dfiltered, dgated = gates(preact, dot_columns(cot[here, :], out_weight[...]))
        mixed_out[at, :] = mixed
        dpre_out[at, :channels] = dfiltered
        dpre_out[at, channels:] = dgated
    dpre = dpre_out[...]
    for k in range(TAPS):
        grad_conv[k * channels : (k + 1) * channels, :] = dot_rows(
            signal[SPAN - k * STEP : rows - k * STEP, :], dpre
        )
    grad_proj[...] = dot_rows(mixed_out[...], cot[SPAN:, :])
    ones = jnp.ones((BIAS_ROWS, rows), BF16)
    grad_bias[:, : 2 * channels] = dot(ones[:, : rows - SPAN], dpre)[:SUBLANES]
    grad_bias[:, 2 * channels :] = dot(ones, cot[...])[:SUBLANES]


def early_kernel(
    level, pieces, history, signal, weight, cot, preact_in, dmixed_in, conv_in, proj_in, bias_in,
    mixed_out, dpre_out, *refs,
):
    radix, digit, core = 1 << len(level), digit_of(level), place_of()[1]
    turn = steps_of(level)
    first = lax.axis_index("tm") == 0
    own, offered = refs[:radix], refs[radix : 2 * radix - 1]
    past, grad_conv, grad_proj = refs[2 * radix - 1 :]
    rows, channels = signal.shape
    tap = lambda k: weight[k * channels : (k + 1) * channels, :]
    past[...] = jnp.where(first, jnp.zeros_like(history), history[...])
    for begin in range(0, SPAN, STEP):
        here = slice(begin, begin + STEP)
        preact = preact_in[here, :]
        for k in range(begin // STEP + 1, TAPS):
            source = SPAN + begin - k * STEP
            preact = preact + dot(past[source : source + STEP, :], tap(k))
        mixed, dfiltered, dgated = gates(preact, dmixed_in[here, :])
        mixed_out[here, :] = mixed
        dpre_out[here, :channels] = dfiltered
        dpre_out[here, channels:] = dgated
    dpre = dpre_out[...]
    for k in range(TAPS):
        at = slice(k * channels, (k + 1) * channels)
        total = conv_in[at, :]
        if k:
            total = total + dot_rows(past[SPAN - k * STEP :, :], dpre[: k * STEP, :])
        if k < TAPS - 1:
            total = total + dot_rows(signal[: SPAN - k * STEP, :], dpre[k * STEP :, :])
        grad_conv[at, :] = total
    grad_proj[: proj_in.shape[0], :] = proj_in[...] + dot_rows(mixed_out[...], cot[:SPAN, :])
    for grad, filled in ((grad_conv, conv_in.shape[0]), (grad_proj, proj_in.shape[0])):
        if filled < grad.shape[0]:
            grad[filled:, :] = jnp.zeros((grad.shape[0] - filled, grad.shape[1]), F32)
    ones = jnp.ones((BIAS_ROWS, SPAN), BF16)
    columns = dot(ones, dpre)[:SUBLANES]
    bias = bias_in[...]
    bias = jnp.concatenate([bias[:, : 2 * channels] + columns, bias[:, 2 * channels :]], 1)
    lines = [bias[:1, c : c + LANES] for c in range(0, bias.shape[1], LANES)]
    lines += [jnp.zeros((1, LANES), F32)] * (SUBLANES - len(lines))
    bias = jnp.concatenate(lines, 0)
    for k in range(radix):
        at = 0
        for piece in range(pieces // radix):
            index = (digit ^ k) * (pieces // radix) + piece
            for grad in (grad_conv, grad_proj):
                height = grad.shape[0] // pieces
                begin = pl.multiple_of(index * height, 16)
                for column in range(0, grad.shape[1], LANES):
                    block = grad[pl.ds(begin, height), column : column + LANES]
                    own[k][at : at + height, :] = block
                    if k in turn[1:]:
                        offered[turn.index(k)][at : at + height, :] = block.astype(BF16)
                    at += height
        own[k][at:, :] = bias
        if k in turn[1:]:
            offered[turn.index(k)][at:, :] = narrowed(bias)
    offered[0][at:, :] = narrowed(bias)
    for mine, k in ((0, 0), (1, turn[0])):

        @pl.when(core == mine)
        def _():
            offered[0][:at, :] = own[k][:at, :].astype(BF16)


def back_kernel(dpre, weight, out):
    channels = out.shape[1]
    tap = lambda k: weight[k * channels : (k + 1) * channels, :]
    for begin in range(0, SPAN, STEP):
        total = dot_columns(dpre[begin : begin + STEP, :], tap(TAPS - 1))
        for k in range(1, TAPS - 1):
            source = begin - SPAN + k * STEP
            if source >= 0:
                total = total + dot_columns(dpre[source : source + STEP, :], tap(k))
        out[begin : begin + STEP, :] = total.astype(BF16)


def own_kernel(signal, weight, out_weight, out_bias, cot, mixed_early, mixed_late, dpre_early, dpre_late, output, partial, token):
    rows, channels = signal.shape
    tap = lambda k: weight[k * channels : (k + 1) * channels, :]
    token[...] = jnp.zeros_like(token)

    def part(early, late, begin):
        ref, at = (early, begin) if begin < SPAN else (late, begin - SPAN)
        return ref[at : at + STEP, :]

    for begin in range(0, rows, STEP):
        here = slice(begin, begin + STEP)
        hidden = dot(part(mixed_early, mixed_late, begin), out_weight[...]) + out_bias[...]
        output[here, :] = (signal[here, :].astype(F32) + hidden).astype(BF16)
        total = cot[here, :].astype(F32)
        for k in range(TAPS):
            if begin + k * STEP < rows:
                total = total + dot_columns(part(dpre_early, dpre_late, begin + k * STEP), tap(k))
        partial[here, :] = total


PLANE = 4


def relay_pairs():
    runs, size = lax.axis_size("run"), lax.axis_size("tm")
    pairs = []
    for t in range(size):
        for r in range(runs):
            to = ((t - PLANE) % size) * runs + r if t % PLANE == 0 else t * runs + (r ^ 1)
            pairs.append((t * runs + r, to))
    return pairs


def plane_pairs():
    size = lax.axis_size("tm")
    return [(t, t - 1 if t % PLANE else t + PLANE - 1) for t in range(size)]


def relay_kernel(back, relayed, onward):
    first = lax.rem(lax.axis_index("tm"), PLANE) == 0
    onward[...] = jnp.where(first, relayed[...], back[...])


def join_kernel(partial, incoming, out, token):
    token[...] = jnp.zeros_like(token)
    rows = partial.shape[0]
    last = lax.axis_index("tm") == lax.axis_size("tm") - 1
    out[: rows - SPAN, :] = partial[: rows - SPAN, :].astype(BF16)
    more = jnp.where(last, jnp.zeros(incoming.shape, F32), incoming[...].astype(F32))
    out[rows - SPAN :, :] = (partial[rows - SPAN :, :] + more).astype(BF16)


def piece_height(rows, pieces):
    return -(-rows // (pieces * 16)) * 16


def widened(block):
    wide = block.astype(F32)
    return wide[:SUBLANES] + wide[SUBLANES:]


def narrowed(total):
    high = total.astype(BF16).astype(F32)
    return jnp.concatenate([high, total - high], 0).astype(BF16)


def first_kernel(keep_own, send_own, received, keep, send):
    end = send.shape[0] - BIAS_ROWS
    more, bias = received[:end, :].astype(F32), widened(received[end:, :])
    keep[:end, :] = keep_own[:end, :] + more
    keep[end:, :] = keep_own[end:, :] + bias
    send[:end, :] = (send_own[:end, :] + more).astype(BF16)
    send[end:, :] = narrowed(send_own[end:, :] + bias)


def next_kernel(send_own, received, send):
    end = send.shape[0] - BIAS_ROWS
    send[:end, :] = (send_own[:end, :] + received[:end, :].astype(F32)).astype(BF16)
    send[end:, :] = narrowed(send_own[end:, :] + widened(received[end:, :]))


def split_kernel(level, more, *refs):
    radix, digit = 1 << len(level), digit_of(level)
    main, received = refs[0], refs[1 : 1 + more]
    sends, keep = refs[1 + more : -1], refs[-1]
    rows, end = sends[0].shape[0] - BIAS_ROWS, main.shape[0] - SUBLANES
    total = main[end:, :]
    for ref in received:
        total = total + widened(ref[end:, :])
    for k in range(radix):
        start = pl.multiple_of((digit ^ k) * rows, 16)
        block = main[pl.ds(start, rows), :]
        for ref in received:
            block = block + ref[pl.ds(start, rows), :].astype(F32)
        if k:
            sends[k - 1][:rows, :] = block.astype(BF16)
            sends[k - 1][rows:, :] = narrowed(total)
        else:
            keep[:rows, :] = block
            keep[rows:, :] = total


def finish_kernel(scale, *refs):
    keep, received, out = refs[0], refs[1:-1], refs[-1]
    rows = out.shape[0] - BIAS_ROWS
    block, total = keep[:rows, :], keep[rows:, :]
    for ref in received:
        block = block + ref[:rows, :].astype(F32)
        total = total + widened(ref[rows:, :])
    out[:rows, :] = (block * scale).astype(BF16)
    out[rows:, :] = narrowed(total * scale)


def place_kernel(level, taker, given, *refs):
    radix, digit, core = 1 << len(level), digit_of(level), place_of()[1]
    parts, out = refs[:radix], refs[radix]
    rows = parts[0].shape[0] - BIAS_ROWS
    own = jnp.where(core == taker, given[...], parts[0][...])
    for k in range(radix):
        block = parts[k][...] if k else own
        index = digit ^ k
        out[pl.ds(pl.multiple_of(index * rows, 16), rows), :] = block[:rows]

        @pl.when(index == 0)
        def _():
            out[radix * rows :, :] = block[rows:]


def copy_kernel(source, out):
    out[...] = source[...]


def spread_kernel(steps, level, taker, pieces, *refs):
    count = len(steps)
    ends = steps[-1] != 0 and count == 1
    digit, core = digit_of(level), place_of()[1]
    direct, passed, refs = refs[:count], refs[count : 2 * count], refs[2 * count :]
    before, refs = (refs[0], refs[3:]) if ends else (None, refs)
    (conv, proj), refs = refs[:2], refs[2:]
    bias_out, (wide_conv, wide_proj, wide_bias, sems) = refs[:-4], refs[-4:]
    bias = before[...] if ends else jnp.zeros((SUBLANES, LANES), F32)
    copies = []

    def send(source, target, *at):
        copies.append(pltpu.make_async_copy(source, target, sems.at[at]))
        copies[-1].start()

    for k, here, there in zip(steps, direct, passed):
        end = here.shape[0] - BIAS_ROWS
        block = jnp.where((core == taker) == (k > 0), here[end:, :], there[end:, :])
        bias = jnp.where((digit ^ k) == 0, widened(block), bias)
    if ends:
        wide_bias[...] = jnp.concatenate([bias[i : i + 1, :] for i in range(SUBLANES)], 1)
        column = 0
        for n, out in enumerate(bias_out):
            send(wide_bias.at[:, column : column + out.shape[1]], out, count, n)
            column += out.shape[1]
    else:
        bias_out[0][...] = bias
    for n, (k, here, there) in enumerate(zip(steps, direct, passed)):
        block = jnp.where((core == taker) == (k > 0), here[...], there[...])
        at = 0
        for piece in range(pieces):
            for wide in (wide_conv, wide_proj):
                height = wide.shape[1] // pieces
                for column in range(0, wide.shape[2], LANES):
                    wide[n, piece * height : (piece + 1) * height, column : column + LANES] = (
                        block[at : at + height].astype(F32)
                    )
                    at += height
        for m, (wide, out) in enumerate(((wide_conv, conv), (wide_proj, proj))):
            height = wide.shape[1]
            start = pl.multiple_of((digit ^ k) * height, 16)
            send(wide.at[n], out.at[pl.ds(start, height), :], n, m)
    for copy in copies:
        copy.wait()


def levels_of(chips):
    count = chips.bit_length() - 1
    bits = list(range(count))
    return [tuple(bits[i : i + 2]) for i in range(0, count, 2)]


def swapped(array):
    chips = count_of_chips()
    return lax.ppermute(array, BOTH, [(i, i ^ 1) for i in range(2 * chips)])


def crossed(array, source, step):
    chips = count_of_chips()
    pairs = [(2 * c + source, 2 * (c ^ step) + 1 - source) for c in range(chips)]
    pairs += [(2 * c + 1 - source, 2 * c + source) for c in range(chips)]
    return lax.ppermute(array, BOTH, pairs)


def summed_everywhere(own, offered, scale, heights, widths, fill):
    chips = count_of_chips()
    levels = levels_of(chips)
    radix, turn = 1 << len(levels[0]), steps_of(levels[0])
    rows = own[0].shape[0] - SUBLANES
    exchanged = [swapped(message) for message in offered]
    keep, send = call(
        first_kernel,
        [held(F32, rows + SUBLANES, LANES), held(BF16, rows + BIAS_ROWS, LANES)],
        (own[0], own[turn[0]], exchanged[0]),
        after=fill(0, ()),
    )
    received = [crossed(send, 0, step_between(levels[0], turn[0]))]
    for k, message in zip(turn[1:], exchanged[1:]):
        (send,) = call(next_kernel, [held(BF16, rows + BIAS_ROWS, LANES)], (own[k], message))
        received.append(crossed(send, 0, step_between(levels[0], k)))
    ready = fill(1, (send,))
    source = 1
    for level in range(1, len(levels)):
        radix = 1 << len(levels[level])
        rows //= radix
        *sends, keep = call(
            functools.partial(split_kernel, levels[level], len(received)),
            [held(BF16, rows + BIAS_ROWS, LANES)] * (radix - 1) + [held(F32, rows + SUBLANES, LANES)],
            (keep, *received),
            after=ready if level == 1 else (),
        )
        if level == 1:
            fill(2, (sends[0],))
        keep = swapped(keep)
        received = [
            crossed(sends[k - 1], source, step_between(levels[level], k))
            for k in steps_of(levels[level])
        ]
        source = 1 - source
    (part,) = call(
        functools.partial(finish_kernel, scale),
        [held(BF16, rows + BIAS_ROWS, LANES)],
        (keep, *received),
        flops=3000000000,
        after=ready if len(levels) == 1 else (),
    )
    if len(levels) == 1:
        fill(2, (part,))
    for level in reversed(range(len(levels))):
        radix = 1 << len(levels[level])
        crossing = {
            k: crossed(part, source, step_between(levels[level], k)) for k in steps_of(levels[level])
        }
        given = swapped(part)
        parts = [part] + [crossing[k] for k in range(1, radix)]
        if level:
            rows = part.shape[0] - BIAS_ROWS
            (part,) = call(
                functools.partial(place_kernel, levels[level], 1 - source),
                [held(BF16, radix * rows + BIAS_ROWS, LANES)],
                (given, *parts),
                after=fill(3, ()) if level == 1 else (),
            )
            source = 1 - source
    taker, pieces = 1 - source, chips // radix
    whole = [shape(F32, chips * h, w) for h, w in zip(heights, widths)]

    def room(count):
        return [
            *[pltpu.VMEM((count, pieces * h, w), F32) for h, w in zip(heights, widths)],
            pltpu.VMEM((1, SUBLANES * LANES), F32),
            pltpu.SemaphoreType.DMA((count + 1, 2)),
        ]

    early, last = [0, *turn[:-1]], turn[-1]
    forwarded = [given]
    for k in early[1:]:
        message = parts[k]
        if k == turn[0]:
            (message,) = call(copy_kernel, [held(BF16, *message.shape)], (message,), after=fill(4, ()))
        forwarded.append(swapped(message))
    conv, proj, bias = call(
        functools.partial(spread_kernel, early, levels[0], taker, pieces),
        whole + [held(F32, SUBLANES, LANES)],
        (*[parts[k] for k in early], *forwarded),
        scratch=room(len(early)),
        far=(-1, -2),
    )
    return call(
        functools.partial(spread_kernel, [last], levels[0], taker, pieces),
        whole + [shape(F32, 1, w) for w in widths],
        (parts[last], swapped(parts[last]), bias, conv, proj),
        scratch=room(1),
        far=(-1, -2, -3, -4, 3, 4),
        alias={3: 0, 4: 1},
    )


def local(signal, conv_weight, conv_bias, out_weight, out_bias, cotangent):
    rows, channels = signal.shape[1:]
    wide = 2 * channels
    late = rows - SPAN
    size = lax.axis_size("tm")
    chips = count_of_chips()
    level = levels_of(chips)[0]
    radix = 1 << len(level)
    widths = (wide, channels)
    heights = [piece_height(n, chips) for n in (TAPS * channels, channels)]
    piece = chips // radix * sum(h * w // LANES for h, w in zip(heights, widths))

    history = lax.ppermute(signal[0, late:], "tm", [(i, (i + 1) % size) for i in range(size)])
    x, weight, proj_weight, cot, preact, dmixed, mixed_late, dpre_late, conv, proj, bias = call(
        late_kernel,
        [
            held(BF16, rows, channels), held(BF16, TAPS * channels, wide), held(BF16, channels, channels),
            held(BF16, rows, channels),
            held(F32, SPAN, wide), held(F32, SPAN, channels), held(BF16, late, channels),
            held(BF16, late, wide), held(F32, TAPS * channels, wide), held(F32, channels, channels),
            held(F32, SUBLANES, wide + channels),
        ],
        (signal[0], conv_weight, conv_bias.reshape(1, -1), out_weight, cotangent[0]),
        scratch=[pltpu.SemaphoreType.DMA((4,))],
        far=(0, 1, 3, 4),
    )
    mixed_early, dpre_early, *pieces = call(
        functools.partial(early_kernel, level, chips),
        [held(BF16, SPAN, channels), held(BF16, SPAN, wide)]
        + [held(F32, piece + SUBLANES, LANES)] * radix
        + [held(BF16, piece + BIAS_ROWS, LANES)] * (radix - 1),
        (
            history, x, weight, cot, preact, dmixed, conv, proj, bias,
        ),
        scratch=[pltpu.VMEM((SPAN, channels), BF16)]
        + [pltpu.VMEM((chips * h, w), F32) for h, w in zip(heights, widths)],
    )
    results = {}

    def fill(stage, after):
        if stage == 0:
            (results["back"],) = call(
                back_kernel, [held(BF16, SPAN, channels)], (dpre_early, weight), after=after
            )
            results["relayed"] = lax.ppermute(results["back"], BOTH, relay_pairs())
            return (results["back"],)
        if stage == 1:
            results["output"], results["partial"], token = call(
                own_kernel,
                [shape(BF16, rows, channels), held(F32, rows, channels), TOKEN],
                (
                    x, weight, proj_weight, out_bias.reshape(1, -1), cot,
                    mixed_early, mixed_late, dpre_early, dpre_late,
                ),
                after=after,
            )
            return (token,)
        if stage == 2:
            (onward,) = call(
                relay_kernel,
                [held(BF16, SPAN, channels)],
                (results["back"], results["relayed"]),
                after=after,
            )
            results["incoming"] = lax.ppermute(onward, "tm", plane_pairs())
            return ()
        if stage == 3:
            return (results["incoming"],)
        results["grad_signal"], token = call(
            join_kernel,
            [shape(BF16, rows, channels), TOKEN],
            (results["partial"], results["incoming"]),
        )
        return (token,)

    scale = float(signal.shape[0] * lax.axis_size("run") * rows * size) ** -0.5
    grad_conv, grad_proj, grad_cbias, grad_pbias = summed_everywhere(
        pieces[:radix], pieces[radix:], scale, heights, widths, fill
    )
    return (
        results["output"][None],
        results["grad_signal"][None],
        grad_conv[: TAPS * channels],
        grad_cbias[0],
        grad_proj[:channels],
        grad_pbias[0],
    )


def solution(mesh):
    placed = (P("run", "tm", None), P(), P(), P(), P(), P("run", "tm", None))
    return jax.shard_map(
        local,
        mesh=mesh,
        in_specs=placed,
        out_specs=(P("run", "tm", None), P("run", "tm", None), P(), P(), P(), P()),
        check_vma=False,
    )
```

```python
import functools

import jax
import jax.numpy as jnp
from jax import lax
from jax.experimental import pallas as pl
from jax.experimental.pallas import tpu as pltpu
from jax.sharding import PartitionSpec as P

STEP = 256
TAPS = 3
SPAN = (TAPS - 1) * STEP
BOTH = ("tm", "run")
LANES = 128
SUBLANES = 8
BIAS_ROWS = 2 * SUBLANES
F32 = jnp.float32
BF16 = jnp.bfloat16
VMEM = pl.BlockSpec(memory_space=pltpu.VMEM)
ANY = pl.BlockSpec(memory_space=pl.ANY)
HBM = pl.BlockSpec(memory_space=pltpu.HBM)
MIB = 1024 * 1024


def call(kernel, out_shape, args, flops=0, scratch=(), after=(), far=(), alias=None):
    moved = sum(a.size * a.dtype.itemsize for a in args)
    inner = kernel
    if after:
        count = len(args)
        inner = lambda *refs: kernel(*refs[:count], *refs[count + len(after) :])
    ins = [HBM if i in far else VMEM for i in range(len(args))]
    outs = [HBM if -1 - i in far else VMEM for i in range(len(out_shape))]
    placed = [
        pltpu.with_memory_space_constraint(a, pltpu.HBM if i in far else pltpu.VMEM)
        for i, a in enumerate(args)
    ]
    return pl.pallas_call(
        inner,
        out_shape=out_shape,
        in_specs=ins + [ANY] * len(after),
        out_specs=outs,
        scratch_shapes=list(scratch),
        input_output_aliases=alias or {},
        cost_estimate=pl.CostEstimate(flops=flops, bytes_accessed=8, transcendentals=0),
        compiler_params=pltpu.CompilerParams(vmem_limit_bytes=(8 if count_of_chips() <= 16 else 40) * MIB),
    )(*placed, *after)


def held(dtype, *dims):
    return pltpu.VMEM(dims, dtype)


def shape(dtype, *dims):
    return jax.ShapeDtypeStruct(dims, dtype)


def count_of_chips():
    return lax.axis_size("tm") * lax.axis_size("run") // 2


def place_of():
    flat = lax.axis_index("tm") * lax.axis_size("run") + lax.axis_index("run")
    return flat // 2, lax.rem(flat, 2)


def digit_of(level):
    chip = place_of()[0]
    return sum(lax.rem(chip // (1 << bit), 2) * (1 << i) for i, bit in enumerate(level))


def steps_of(level):
    last = (1 << len(level)) - 1
    return [last, *range(1, last)]


def step_between(level, k):
    return sum(1 << bit for i, bit in enumerate(level) if k >> i & 1)


TOKEN = held(F32, SUBLANES, LANES)


def dot(a, b):
    return jnp.dot(a, b, preferred_element_type=F32)


def dot_rows(a, b):
    return lax.dot_general(a, b, (((0,), (0,)), ((), ())), preferred_element_type=F32)


def dot_columns(a, b):
    return lax.dot_general(a, b, (((1,), (1,)), ((), ())), preferred_element_type=F32)


def gates(preact, dmixed):
    channels = dmixed.shape[1]
    filtered = jnp.tanh(preact[:, :channels])
    gated = jax.nn.sigmoid(preact[:, channels:])
    mixed = filtered * gated
    dfiltered = dmixed * gated * (1.0 - filtered * filtered)
    dgated = dmixed * mixed * (1.0 - gated)
    return mixed.astype(BF16), dfiltered.astype(BF16), dgated.astype(BF16)


def late_kernel(
    signal_in, weight_in, bias, out_weight_in, cot_in,
    signal, weight, out_weight, cot,
    preact_out, dmixed_out, mixed_out, dpre_out, grad_conv, grad_proj, grad_bias, sems,
):
    rows, channels = signal.shape
    pairs = ((signal_in, signal), (weight_in, weight), (cot_in, cot), (out_weight_in, out_weight))
    copies = [pltpu.make_async_copy(a, b, sems.at[i]) for i, (a, b) in enumerate(pairs)]
    for copy in copies:
        copy.start()
    tap = lambda k: weight[k * channels : (k + 1) * channels, :]
    copies[0].wait()
    copies[1].wait()
    preact_out[...] = dot(signal[:SPAN, :], tap(0)) + bias[...]
    for k in range(1, TAPS - 1):
        preact_out[k * STEP :, :] += dot(signal[: SPAN - k * STEP, :], tap(k))
    copies[2].wait()
    copies[3].wait()
    dmixed_out[...] = dot_columns(cot[:SPAN, :], out_weight[...])
    for begin in range(SPAN, rows, STEP):
        here = slice(begin, begin + STEP)
        at = slice(begin - SPAN, begin - SPAN + STEP)
        preact = bias[...]
        for k in range(TAPS):
            preact = preact + dot(signal[begin - k * STEP : begin - k * STEP + STEP, :], tap(k))
        mixed, dfiltered, dgated = gates(preact, dot_columns(cot[here, :], out_weight[...]))
        mixed_out[at, :] = mixed
        dpre_out[at, :channels] = dfiltered
        dpre_out[at, channels:] = dgated
    dpre = dpre_out[...]
    for k in range(TAPS):
        grad_conv[k * channels : (k + 1) * channels, :] = dot_rows(
            signal[SPAN - k * STEP : rows - k * STEP, :], dpre
        )
    grad_proj[...] = dot_rows(mixed_out[...], cot[SPAN:, :])
    ones = jnp.ones((BIAS_ROWS, rows), BF16)
    grad_bias[:, : 2 * channels] = dot(ones[:, : rows - SPAN], dpre)[:SUBLANES]
    grad_bias[:, 2 * channels :] = dot(ones, cot[...])[:SUBLANES]


def chunk(begin, past, signal, weight, cot, preact_in, dmixed_in, conv_in, proj_in, bias_in, mixed_out, dpre_out, conv, proj):
    channels = signal.shape[1]
    here = slice(begin, begin + STEP)
    own = begin // STEP + 1
    past = [
        jnp.where(lax.axis_index("tm") == 0, jnp.zeros_like(block), block[...]) for block in past
    ]
    preact = preact_in[here, :]
    for k in range(own, TAPS):
        preact = preact + dot(past[k - own], weight[k * channels : (k + 1) * channels, :])
    mixed, dfiltered, dgated = gates(preact, dmixed_in[here, :])
    mixed_out[...] = mixed
    dpre_out[:, :channels] = dfiltered
    dpre_out[:, channels:] = dgated
    dpre = dpre_out[...]
    for k in range(TAPS):
        at = slice(k * channels, (k + 1) * channels)
        seen = past[k - own] if k >= own else signal[begin - k * STEP : begin - k * STEP + STEP, :]
        conv[at, :] = conv_in[at, :] + dot_rows(seen, dpre)
    proj[: channels, :] = proj_in[...] + dot_rows(mixed, cot[here, :])
    columns = dot(jnp.ones((BIAS_ROWS, STEP), BF16), dpre)[:SUBLANES]
    return jnp.concatenate([bias_in[:, : 2 * channels] + columns, bias_in[:, 2 * channels :]], 1)


def middle_kernel(begin, *refs):
    *ins, grad_bias = refs
    grad_bias[...] = chunk(begin, ins[:1], *ins[1:])


def early_kernel(level, pieces, *refs):
    radix, digit, core = 1 << len(level), digit_of(level), place_of()[1]
    turn = steps_of(level)
    ins, (mixed_out, dpre_out), refs = refs[: TAPS + 7], refs[TAPS + 7 : TAPS + 9], refs[TAPS + 9 :]
    own, offered = refs[:radix], refs[radix : 2 * radix - 1]
    grad_conv, grad_proj = refs[2 * radix - 1 :]
    bias = chunk(0, ins[: TAPS - 1], *ins[TAPS - 1 :], mixed_out, dpre_out, grad_conv, grad_proj)
    conv_in, proj_in = ins[-3], ins[-2]
    for grad, filled in ((grad_conv, conv_in.shape[0]), (grad_proj, proj_in.shape[0])):
        if filled < grad.shape[0]:
            grad[filled:, :] = jnp.zeros((grad.shape[0] - filled, grad.shape[1]), F32)
    lines = [bias[:1, c : c + LANES] for c in range(0, bias.shape[1], LANES)]
    lines += [jnp.zeros((1, LANES), F32)] * (SUBLANES - len(lines))
    bias = jnp.concatenate(lines, 0)
    for k in range(radix):
        at = 0
        for piece in range(pieces // radix):
            index = (digit ^ k) * (pieces // radix) + piece
            for grad in (grad_conv, grad_proj):
                height = grad.shape[0] // pieces
                begin = pl.multiple_of(index * height, 16)
                for column in range(0, grad.shape[1], LANES):
                    block = grad[pl.ds(begin, height), column : column + LANES]
                    own[k][at : at + height, :] = block
                    if k in turn[1:]:
                        offered[turn.index(k)][at : at + height, :] = block.astype(BF16)
                    at += height
        own[k][at:, :] = bias
        if k in turn[1:]:
            offered[turn.index(k)][at:, :] = narrowed(bias)
    offered[0][at:, :] = narrowed(bias)
    for mine, k in ((0, 0), (1, turn[0])):

        @pl.when(core == mine)
        def _():
            offered[0][:at, :] = own[k][:at, :].astype(BF16)


def back_kernel(*refs):
    *blocks, weight, out = refs
    channels = out.shape[1]
    tap = lambda k: weight[k * channels : (k + 1) * channels, :]
    for n in range(TAPS - 1):
        total = dot_columns(blocks[n][...], tap(TAPS - 1))
        for k in range(TAPS - 1 - n, TAPS - 1):
            total = total + dot_columns(blocks[n - TAPS + 1 + k][...], tap(k))
        out[n * STEP : (n + 1) * STEP, :] = total.astype(BF16)


def own_kernel(signal, weight, out_weight, out_bias, cot, *refs):
    rows, channels = signal.shape
    tap = lambda k: weight[k * channels : (k + 1) * channels, :]
    mixed, dpre, (output, partial, token) = refs[:TAPS], refs[TAPS : 2 * TAPS], refs[2 * TAPS :]
    token[...] = jnp.zeros_like(token)

    def part(refs, begin):
        block = min(begin // STEP, TAPS - 1)
        return refs[block][begin - block * STEP : begin - block * STEP + STEP, :]

    for begin in range(0, rows, STEP):
        here = slice(begin, begin + STEP)
        hidden = dot(part(mixed, begin), out_weight[...]) + out_bias[...]
        output[here, :] = (signal[here, :].astype(F32) + hidden).astype(BF16)
        total = cot[here, :].astype(F32)
        for k in range(TAPS):
            if begin + k * STEP < rows:
                total = total + dot_columns(part(dpre, begin + k * STEP), tap(k))
        partial[here, :] = total


PLANE = 4


def relay_pairs():
    runs, size = lax.axis_size("run"), lax.axis_size("tm")
    pairs = []
    for t in range(size):
        for r in range(runs):
            to = ((t - PLANE) % size) * runs + r if t % PLANE == 0 else t * runs + (r ^ 1)
            pairs.append((t * runs + r, to))
    return pairs


def plane_pairs():
    size = lax.axis_size("tm")
    return [(t, t - 1 if t % PLANE else t + PLANE - 1) for t in range(size)]


def relay_kernel(back, relayed, onward):
    first = lax.rem(lax.axis_index("tm"), PLANE) == 0
    onward[...] = jnp.where(first, relayed[...], back[...])


def join_kernel(partial, incoming, out, token):
    token[...] = jnp.zeros_like(token)
    rows = partial.shape[0]
    last = lax.axis_index("tm") == lax.axis_size("tm") - 1
    out[: rows - SPAN, :] = partial[: rows - SPAN, :].astype(BF16)
    more = jnp.where(last, jnp.zeros(incoming.shape, F32), incoming[...].astype(F32))
    out[rows - SPAN :, :] = (partial[rows - SPAN :, :] + more).astype(BF16)


def piece_height(rows, pieces):
    return -(-rows // (pieces * 16)) * 16


def widened(block):
    wide = block.astype(F32)
    return wide[:SUBLANES] + wide[SUBLANES:]


def narrowed(total):
    high = total.astype(BF16).astype(F32)
    return jnp.concatenate([high, total - high], 0).astype(BF16)


def first_kernel(keep_own, send_own, received, keep, send):
    end = send.shape[0] - BIAS_ROWS
    more, bias = received[:end, :].astype(F32), widened(received[end:, :])
    keep[:end, :] = keep_own[:end, :] + more
    keep[end:, :] = keep_own[end:, :] + bias
    send[:end, :] = (send_own[:end, :] + more).astype(BF16)
    send[end:, :] = narrowed(send_own[end:, :] + bias)


def next_kernel(send_own, received, send):
    end = send.shape[0] - BIAS_ROWS
    send[:end, :] = (send_own[:end, :] + received[:end, :].astype(F32)).astype(BF16)
    send[end:, :] = narrowed(send_own[end:, :] + widened(received[end:, :]))


def split_kernel(level, more, *refs):
    radix, digit = 1 << len(level), digit_of(level)
    main, received = refs[0], refs[1 : 1 + more]
    sends, keep = refs[1 + more : -1], refs[-1]
    rows, end = sends[0].shape[0] - BIAS_ROWS, main.shape[0] - SUBLANES
    total = main[end:, :]
    for ref in received:
        total = total + widened(ref[end:, :])
    for k in range(radix):
        start = pl.multiple_of((digit ^ k) * rows, 16)
        block = main[pl.ds(start, rows), :]
        for ref in received:
            block = block + ref[pl.ds(start, rows), :].astype(F32)
        if k:
            sends[k - 1][:rows, :] = block.astype(BF16)
            sends[k - 1][rows:, :] = narrowed(total)
        else:
            keep[:rows, :] = block
            keep[rows:, :] = total


def finish_kernel(scale, *refs):
    keep, received, out = refs[0], refs[1:-1], refs[-1]
    rows = out.shape[0] - BIAS_ROWS
    block, total = keep[:rows, :], keep[rows:, :]
    for ref in received:
        block = block + ref[:rows, :].astype(F32)
        total = total + widened(ref[rows:, :])
    out[:rows, :] = (block * scale).astype(BF16)
    out[rows:, :] = narrowed(total * scale)


def place_kernel(level, taker, given, *refs):
    radix, digit, core = 1 << len(level), digit_of(level), place_of()[1]
    parts, out = refs[:radix], refs[radix]
    rows = parts[0].shape[0] - BIAS_ROWS
    own = jnp.where(core == taker, given[...], parts[0][...])
    for k in range(radix):
        block = parts[k][...] if k else own
        index = digit ^ k
        out[pl.ds(pl.multiple_of(index * rows, 16), rows), :] = block[:rows]

        @pl.when(index == 0)
        def _():
            out[radix * rows :, :] = block[rows:]


def copy_kernel(source, out):
    out[...] = source[...]


def spread_kernel(steps, level, taker, pieces, *refs):
    count = len(steps)
    ends = steps[-1] != 0 and count == 1
    digit, core = digit_of(level), place_of()[1]
    direct, passed, refs = refs[:count], refs[count : 2 * count], refs[2 * count :]
    before, refs = (refs[0], refs[3:]) if ends else (None, refs)
    (conv, proj), refs = refs[:2], refs[2:]
    bias_out, (wide_conv, wide_proj, wide_bias, sems) = refs[:-4], refs[-4:]
    bias = before[...] if ends else jnp.zeros((SUBLANES, LANES), F32)
    copies = []

    def send(source, target, *at):
        copies.append(pltpu.make_async_copy(source, target, sems.at[at]))
        copies[-1].start()

    for k, here, there in zip(steps, direct, passed):
        end = here.shape[0] - BIAS_ROWS
        block = jnp.where((core == taker) == (k > 0), here[end:, :], there[end:, :])
        bias = jnp.where((digit ^ k) == 0, widened(block), bias)
    if ends:
        wide_bias[...] = jnp.concatenate([bias[i : i + 1, :] for i in range(SUBLANES)], 1)
        column = 0
        for n, out in enumerate(bias_out):
            send(wide_bias.at[:, column : column + out.shape[1]], out, count, n)
            column += out.shape[1]
    else:
        bias_out[0][...] = bias
    for n, (k, here, there) in enumerate(zip(steps, direct, passed)):
        block = jnp.where((core == taker) == (k > 0), here[...], there[...])
        at = 0
        for piece in range(pieces):
            for wide in (wide_conv, wide_proj):
                height = wide.shape[1] // pieces
                for column in range(0, wide.shape[2], LANES):
                    wide[n, piece * height : (piece + 1) * height, column : column + LANES] = (
                        block[at : at + height].astype(F32)
                    )
                    at += height
        for m, (wide, out) in enumerate(((wide_conv, conv), (wide_proj, proj))):
            height = wide.shape[1]
            start = pl.multiple_of((digit ^ k) * height, 16)
            send(wide.at[n], out.at[pl.ds(start, height), :], n, m)
    for copy in copies:
        copy.wait()


def levels_of(chips):
    count = chips.bit_length() - 1
    bits = list(range(count))
    return [tuple(bits[i : i + 2]) for i in range(0, count, 2)]


def swapped(array):
    chips = count_of_chips()
    return lax.ppermute(array, BOTH, [(i, i ^ 1) for i in range(2 * chips)])


def crossed(array, source, step):
    chips = count_of_chips()
    pairs = [(2 * c + source, 2 * (c ^ step) + 1 - source) for c in range(chips)]
    pairs += [(2 * c + 1 - source, 2 * c + source) for c in range(chips)]
    return lax.ppermute(array, BOTH, pairs)


def summed_everywhere(own, offered, scale, heights, widths, fill):
    chips = count_of_chips()
    levels = levels_of(chips)
    radix, turn = 1 << len(levels[0]), steps_of(levels[0])
    rows = own[0].shape[0] - SUBLANES
    exchanged = [swapped(message) for message in offered]
    keep, send = call(
        first_kernel,
        [held(F32, rows + SUBLANES, LANES), held(BF16, rows + BIAS_ROWS, LANES)],
        (own[0], own[turn[0]], exchanged[0]),
        after=fill(0, ()),
    )
    received = [crossed(send, 0, step_between(levels[0], turn[0]))]
    for k, message in zip(turn[1:], exchanged[1:]):
        (send,) = call(next_kernel, [held(BF16, rows + BIAS_ROWS, LANES)], (own[k], message))
        received.append(crossed(send, 0, step_between(levels[0], k)))
    ready = fill(1, (send,))
    source = 1
    for level in range(1, len(levels)):
        radix = 1 << len(levels[level])
        rows //= radix
        *sends, keep = call(
            functools.partial(split_kernel, levels[level], len(received)),
            [held(BF16, rows + BIAS_ROWS, LANES)] * (radix - 1) + [held(F32, rows + SUBLANES, LANES)],
            (keep, *received),
            after=ready if level == 1 else (),
        )
        if level == 1:
            fill(2, (sends[0],))
        keep = swapped(keep)
        received = [
            crossed(sends[k - 1], source, step_between(levels[level], k))
            for k in steps_of(levels[level])
        ]
        source = 1 - source
    (part,) = call(
        functools.partial(finish_kernel, scale),
        [held(BF16, rows + BIAS_ROWS, LANES)],
        (keep, *received),
        flops=3000000000,
        after=ready if len(levels) == 1 else (),
    )
    if len(levels) == 1:
        fill(2, (part,))
    for level in reversed(range(len(levels))):
        radix = 1 << len(levels[level])
        crossing = {
            k: crossed(part, source, step_between(levels[level], k)) for k in steps_of(levels[level])
        }
        given = swapped(part)
        parts = [part] + [crossing[k] for k in range(1, radix)]
        if level:
            rows = part.shape[0] - BIAS_ROWS
            (part,) = call(
                functools.partial(place_kernel, levels[level], 1 - source),
                [held(BF16, radix * rows + BIAS_ROWS, LANES)],
                (given, *parts),
                after=fill(3, ()) if level == 1 else (),
            )
            source = 1 - source
    taker, pieces = 1 - source, chips // radix
    whole = [shape(F32, chips * h, w) for h, w in zip(heights, widths)]

    def room(count):
        return [
            *[pltpu.VMEM((count, pieces * h, w), F32) for h, w in zip(heights, widths)],
            pltpu.VMEM((1, SUBLANES * LANES), F32),
            pltpu.SemaphoreType.DMA((count + 1, 2)),
        ]

    early, last = [0, *turn[:-1]], turn[-1]
    forwarded = [given]
    for k in early[1:]:
        message = parts[k]
        if k == turn[0]:
            (message,) = call(copy_kernel, [held(BF16, *message.shape)], (message,), after=fill(4, ()))
        forwarded.append(swapped(message))
    conv, proj, bias = call(
        functools.partial(spread_kernel, early, levels[0], taker, pieces),
        whole + [held(F32, SUBLANES, LANES)],
        (*[parts[k] for k in early], *forwarded),
        scratch=room(len(early)),
        far=(-1, -2),
    )
    return call(
        functools.partial(spread_kernel, [last], levels[0], taker, pieces),
        whole + [shape(F32, 1, w) for w in widths],
        (parts[last], swapped(parts[last]), bias, conv, proj),
        scratch=room(1),
        far=(-1, -2, -3, -4, 3, 4),
        alias={3: 0, 4: 1},
    )


def local(signal, conv_weight, conv_bias, out_weight, out_bias, cotangent):
    rows, channels = signal.shape[1:]
    wide = 2 * channels
    late = rows - SPAN
    size = lax.axis_size("tm")
    chips = count_of_chips()
    level = levels_of(chips)[0]
    radix = 1 << len(level)
    widths = (wide, channels)
    heights = [piece_height(n, chips) for n in (TAPS * channels, channels)]
    piece = chips // radix * sum(h * w // LANES for h, w in zip(heights, widths))

    history = [
        lax.ppermute(
            signal[0, rows - n * STEP : rows - n * STEP + STEP],
            "tm",
            [(i, (i + 1) % size) for i in range(size)],
        )
        for n in range(1, TAPS)
    ]
    x, weight, proj_weight, cot, preact, dmixed, mixed_late, dpre_late, conv, proj, bias = call(
        late_kernel,
        [
            held(BF16, rows, channels), held(BF16, TAPS * channels, wide), held(BF16, channels, channels),
            held(BF16, rows, channels),
            held(F32, SPAN, wide), held(F32, SPAN, channels), held(BF16, late, channels),
            held(BF16, late, wide), held(F32, TAPS * channels, wide), held(F32, channels, channels),
            held(F32, SUBLANES, wide + channels),
        ],
        (signal[0], conv_weight, conv_bias.reshape(1, -1), out_weight, cotangent[0]),
        scratch=[pltpu.SemaphoreType.DMA((4,))],
        far=(0, 1, 3, 4),
    )
    grads = [held(F32, TAPS * channels, wide), held(F32, channels, channels)]
    mixed_middle, dpre_middle, conv, proj, bias = call(
        functools.partial(middle_kernel, STEP),
        [held(BF16, STEP, channels), held(BF16, STEP, wide), *grads, held(F32, SUBLANES, wide + channels)],
        (history[0], x, weight, cot, preact, dmixed, conv, proj, bias),
    )
    mixed_early, dpre_early, *pieces = call(
        functools.partial(early_kernel, level, chips),
        [held(BF16, STEP, channels), held(BF16, STEP, wide)]
        + [held(F32, piece + SUBLANES, LANES)] * radix
        + [held(BF16, piece + BIAS_ROWS, LANES)] * (radix - 1),
        (*history, x, weight, cot, preact, dmixed, conv, proj, bias),
        scratch=[pltpu.VMEM((chips * h, w), F32) for h, w in zip(heights, widths)],
    )
    results = {}

    def fill(stage, after):
        if stage == 0:
            (results["back"],) = call(
                back_kernel, [held(BF16, SPAN, channels)], (dpre_early, dpre_middle, weight), after=after
            )
            results["relayed"] = lax.ppermute(results["back"], BOTH, relay_pairs())
            return (results["back"],)
        if stage == 1:
            results["output"], results["partial"], token = call(
                own_kernel,
                [shape(BF16, rows, channels), held(F32, rows, channels), TOKEN],
                (
                    x, weight, proj_weight, out_bias.reshape(1, -1), cot,
                    mixed_early, mixed_middle, mixed_late, dpre_early, dpre_middle, dpre_late,
                ),
                after=after,
            )
            return (token,)
        if stage == 2:
            (onward,) = call(
                relay_kernel,
                [held(BF16, SPAN, channels)],
                (results["back"], results["relayed"]),
                after=after,
            )
            results["incoming"] = lax.ppermute(onward, "tm", plane_pairs())
            return ()
        if stage == 3:
            return (results["incoming"],)
        results["grad_signal"], token = call(
            join_kernel,
            [shape(BF16, rows, channels), TOKEN],
            (results["partial"], results["incoming"]),
        )
        return (token,)

    scale = float(signal.shape[0] * lax.axis_size("run") * rows * size) ** -0.5
    grad_conv, grad_proj, grad_cbias, grad_pbias = summed_everywhere(
        pieces[:radix], pieces[radix:], scale, heights, widths, fill
    )
    return (
        results["output"][None],
        results["grad_signal"][None],
        grad_conv[: TAPS * channels],
        grad_cbias[0],
        grad_proj[:channels],
        grad_pbias[0],
    )


def solution(mesh):
    placed = (P("run", "tm", None), P(), P(), P(), P(), P("run", "tm", None))
    return jax.shard_map(
        local,
        mesh=mesh,
        in_specs=placed,
        out_specs=(P("run", "tm", None), P("run", "tm", None), P(), P(), P(), P()),
        check_vma=False,
    )
```

```python
import functools

import jax
import jax.numpy as jnp
from jax import lax
from jax.experimental import pallas as pl
from jax.experimental.pallas import tpu as pltpu
from jax.sharding import PartitionSpec as P

STEP = 256
TAPS = 3
SPAN = (TAPS - 1) * STEP
BOTH = ("tm", "run")
LANES = 128
SUBLANES = 8
BIAS_ROWS = 2 * SUBLANES
F32 = jnp.float32
BF16 = jnp.bfloat16
VMEM = pl.BlockSpec(memory_space=pltpu.VMEM)
ANY = pl.BlockSpec(memory_space=pl.ANY)
HBM = pl.BlockSpec(memory_space=pltpu.HBM)
MIB = 1024 * 1024


def call(kernel, out_shape, args, flops=0, scratch=(), after=(), far=(), alias=None):
    moved = sum(a.size * a.dtype.itemsize for a in args)
    inner = kernel
    if after:
        count = len(args)
        inner = lambda *refs: kernel(*refs[:count], *refs[count + len(after) :])
    ins = [HBM if i in far else VMEM for i in range(len(args))]
    outs = [HBM if -1 - i in far else VMEM for i in range(len(out_shape))]
    placed = [
        pltpu.with_memory_space_constraint(a, pltpu.HBM if i in far else pltpu.VMEM)
        for i, a in enumerate(args)
    ]
    return pl.pallas_call(
        inner,
        out_shape=out_shape,
        in_specs=ins + [ANY] * len(after),
        out_specs=outs,
        scratch_shapes=list(scratch),
        input_output_aliases=alias or {},
        cost_estimate=pl.CostEstimate(flops=flops, bytes_accessed=8, transcendentals=0),
        compiler_params=pltpu.CompilerParams(vmem_limit_bytes=(8 if count_of_chips() <= 16 else 40) * MIB),
    )(*placed, *after)


def held(dtype, *dims):
    return pltpu.VMEM(dims, dtype)


def shape(dtype, *dims):
    return jax.ShapeDtypeStruct(dims, dtype)


def count_of_chips():
    return lax.axis_size("tm") * lax.axis_size("run") // 2


def place_of():
    flat = lax.axis_index("tm") * lax.axis_size("run") + lax.axis_index("run")
    return flat // 2, lax.rem(flat, 2)


def digit_of(level):
    chip = place_of()[0]
    return sum(lax.rem(chip // (1 << bit), 2) * (1 << i) for i, bit in enumerate(level))


def steps_of(level):
    last = (1 << len(level)) - 1
    return [last, *range(1, last)]


def step_between(level, k):
    return sum(1 << bit for i, bit in enumerate(level) if k >> i & 1)


TOKEN = held(F32, SUBLANES, LANES)


def dot(a, b):
    return jnp.dot(a, b, preferred_element_type=F32)


def dot_rows(a, b):
    return lax.dot_general(a, b, (((0,), (0,)), ((), ())), preferred_element_type=F32)


def dot_columns(a, b):
    return lax.dot_general(a, b, (((1,), (1,)), ((), ())), preferred_element_type=F32)


def gates(preact, dmixed):
    channels = dmixed.shape[1]
    filtered = jnp.tanh(preact[:, :channels])
    gated = jax.nn.sigmoid(preact[:, channels:])
    mixed = filtered * gated
    dfiltered = dmixed * gated * (1.0 - filtered * filtered)
    dgated = dmixed * mixed * (1.0 - gated)
    return mixed.astype(BF16), dfiltered.astype(BF16), dgated.astype(BF16)


def late_kernel(
    signal_in, weight_in, bias, out_weight_in, cot_in,
    signal, weight, out_weight, cot,
    preact_out, dmixed_out, mixed_out, dpre_out, grad_conv, grad_proj, grad_bias, sems,
):
    rows, channels = signal.shape
    pairs = ((signal_in, signal), (weight_in, weight), (cot_in, cot), (out_weight_in, out_weight))
    copies = [pltpu.make_async_copy(a, b, sems.at[i]) for i, (a, b) in enumerate(pairs)]
    for copy in copies:
        copy.start()
    tap = lambda k: weight[k * channels : (k + 1) * channels, :]
    copies[0].wait()
    copies[1].wait()
    preact_out[...] = dot(signal[:SPAN, :], tap(0)) + bias[...]
    for k in range(1, TAPS - 1):
        preact_out[k * STEP :, :] += dot(signal[: SPAN - k * STEP, :], tap(k))
    copies[2].wait()
    copies[3].wait()
    dmixed_out[...] = dot_columns(cot[:SPAN, :], out_weight[...])
    for begin in range(SPAN, rows, STEP):
        here = slice(begin, begin + STEP)
        at = slice(begin - SPAN, begin - SPAN + STEP)
        preact = bias[...]
        for k in range(TAPS):
            preact = preact + dot(signal[begin - k * STEP : begin - k * STEP + STEP, :], tap(k))
        mixed, dfiltered, dgated = gates(preact, dot_columns(cot[here, :], out_weight[...]))
        mixed_out[at, :] = mixed
        dpre_out[at, :channels] = dfiltered
        dpre_out[at, channels:] = dgated
    dpre = dpre_out[...]
    for k in range(TAPS):
        grad_conv[k * channels : (k + 1) * channels, :] = dot_rows(
            signal[SPAN - k * STEP : rows - k * STEP, :], dpre
        )
    grad_proj[...] = dot_rows(mixed_out[...], cot[SPAN:, :])
    ones = jnp.ones((BIAS_ROWS, rows), BF16)
    grad_bias[:, : 2 * channels] = dot(ones[:, : rows - SPAN], dpre)[:SUBLANES]
    grad_bias[:, 2 * channels :] = dot(ones, cot[...])[:SUBLANES]


def chunk(begin, past, signal, weight, cot, preact_in, dmixed_in, conv_in, proj_in, bias_in, mixed_out, dpre_out, conv, proj):
    channels = signal.shape[1]
    here = slice(begin, begin + STEP)
    own = begin // STEP + 1
    past = [
        jnp.where(lax.axis_index("tm") == 0, jnp.zeros_like(block), block[...]) for block in past
    ]
    preact = preact_in[here, :]
    for k in range(own, TAPS):
        preact = preact + dot(past[k - own], weight[k * channels : (k + 1) * channels, :])
    mixed, dfiltered, dgated = gates(preact, dmixed_in[here, :])
    mixed_out[...] = mixed
    dpre_out[:, :channels] = dfiltered
    dpre_out[:, channels:] = dgated
    dpre = dpre_out[...]
    for k in range(TAPS):
        at = slice(k * channels, (k + 1) * channels)
        seen = past[k - own] if k >= own else signal[begin - k * STEP : begin - k * STEP + STEP, :]
        conv[at, :] = conv_in[at, :] + dot_rows(seen, dpre)
    proj[: channels, :] = proj_in[...] + dot_rows(mixed, cot[here, :])
    columns = dot(jnp.ones((BIAS_ROWS, STEP), BF16), dpre)[:SUBLANES]
    return jnp.concatenate([bias_in[:, : 2 * channels] + columns, bias_in[:, 2 * channels :]], 1)


def middle_kernel(begin, *refs):
    *ins, grad_bias = refs
    grad_bias[...] = chunk(begin, ins[:1], *ins[1:])


def early_kernel(level, pieces, *refs):
    radix, digit, core = 1 << len(level), digit_of(level), place_of()[1]
    turn = steps_of(level)
    ins, (mixed_out, dpre_out), refs = refs[: TAPS + 7], refs[TAPS + 7 : TAPS + 9], refs[TAPS + 9 :]
    own, offered = refs[:radix], refs[radix : 2 * radix - 1]
    grad_conv, grad_proj = refs[2 * radix - 1 :]
    bias = chunk(0, ins[: TAPS - 1], *ins[TAPS - 1 :], mixed_out, dpre_out, grad_conv, grad_proj)
    conv_in, proj_in = ins[-3], ins[-2]
    for grad, filled in ((grad_conv, conv_in.shape[0]), (grad_proj, proj_in.shape[0])):
        if filled < grad.shape[0]:
            grad[filled:, :] = jnp.zeros((grad.shape[0] - filled, grad.shape[1]), F32)
    lines = [bias[:1, c : c + LANES] for c in range(0, bias.shape[1], LANES)]
    lines += [jnp.zeros((1, LANES), F32)] * (SUBLANES - len(lines))
    bias = jnp.concatenate(lines, 0)
    for k in range(radix):
        at = 0
        for piece in range(pieces // radix):
            index = (digit ^ k) * (pieces // radix) + piece
            for grad in (grad_conv, grad_proj):
                height = grad.shape[0] // pieces
                begin = pl.multiple_of(index * height, 16)
                for column in range(0, grad.shape[1], LANES):
                    block = grad[pl.ds(begin, height), column : column + LANES]
                    own[k][at : at + height, :] = block
                    if k in turn[1:]:
                        offered[turn.index(k)][at : at + height, :] = block.astype(BF16)
                    at += height
        own[k][at:, :] = bias
        if k in turn[1:]:
            offered[turn.index(k)][at:, :] = narrowed(bias)
    offered[0][at:, :] = narrowed(bias)
    for mine, k in ((0, 0), (1, turn[0])):

        @pl.when(core == mine)
        def _():
            offered[0][:at, :] = own[k][:at, :].astype(BF16)


def back_kernel(*refs):
    *blocks, weight, out = refs
    channels = out.shape[1]
    tap = lambda k: weight[k * channels : (k + 1) * channels, :]
    for n in range(TAPS - 1):
        total = dot_columns(blocks[n][...], tap(TAPS - 1))
        for k in range(TAPS - 1 - n, TAPS - 1):
            total = total + dot_columns(blocks[n - TAPS + 1 + k][...], tap(k))
        out[n * STEP : (n + 1) * STEP, :] = total.astype(BF16)


def own_kernel(signal, weight, out_weight, out_bias, cot, *refs):
    rows, channels = signal.shape
    tap = lambda k: weight[k * channels : (k + 1) * channels, :]
    mixed, dpre, (output, partial, token) = refs[:TAPS], refs[TAPS : 2 * TAPS], refs[2 * TAPS :]
    token[...] = jnp.zeros_like(token)

    def part(refs, begin):
        block = min(begin // STEP, TAPS - 1)
        return refs[block][begin - block * STEP : begin - block * STEP + STEP, :]

    for begin in range(0, rows, STEP):
        here = slice(begin, begin + STEP)
        hidden = dot(part(mixed, begin), out_weight[...]) + out_bias[...]
        output[here, :] = (signal[here, :].astype(F32) + hidden).astype(BF16)
        total = cot[here, :].astype(F32)
        for k in range(TAPS):
            if begin + k * STEP < rows:
                total = total + dot_columns(part(dpre, begin + k * STEP), tap(k))
        partial[here, :] = total


PLANE = 4


def relay_pairs():
    runs, size = lax.axis_size("run"), lax.axis_size("tm")
    pairs = []
    for t in range(size):
        for r in range(runs):
            to = ((t - PLANE) % size) * runs + r if t % PLANE == 0 else t * runs + (r ^ 1)
            pairs.append((t * runs + r, to))
    return pairs


def plane_pairs():
    size = lax.axis_size("tm")
    return [(t, t - 1 if t % PLANE else t + PLANE - 1) for t in range(size)]


def relay_kernel(back, relayed, onward):
    first = lax.rem(lax.axis_index("tm"), PLANE) == 0
    onward[...] = jnp.where(first, relayed[...], back[...])


def join_kernel(partial, incoming, out, token):
    token[...] = jnp.zeros_like(token)
    rows = partial.shape[0]
    last = lax.axis_index("tm") == lax.axis_size("tm") - 1
    out[: rows - SPAN, :] = partial[: rows - SPAN, :].astype(BF16)
    more = jnp.where(last, jnp.zeros(incoming.shape, F32), incoming[...].astype(F32))
    out[rows - SPAN :, :] = (partial[rows - SPAN :, :] + more).astype(BF16)


def piece_height(rows, pieces):
    return -(-rows // (pieces * 16)) * 16


def widened(block):
    wide = block.astype(F32)
    return wide[:SUBLANES] + wide[SUBLANES:]


def narrowed(total):
    high = total.astype(BF16).astype(F32)
    return jnp.concatenate([high, total - high], 0).astype(BF16)


def first_kernel(keep_own, send_own, received, keep, send):
    end = send.shape[0] - BIAS_ROWS
    more, bias = received[:end, :].astype(F32), widened(received[end:, :])
    keep[:end, :] = keep_own[:end, :] + more
    keep[end:, :] = keep_own[end:, :] + bias
    send[:end, :] = (send_own[:end, :] + more).astype(BF16)
    send[end:, :] = narrowed(send_own[end:, :] + bias)


def next_kernel(send_own, received, send):
    end = send.shape[0] - BIAS_ROWS
    send[:end, :] = (send_own[:end, :] + received[:end, :].astype(F32)).astype(BF16)
    send[end:, :] = narrowed(send_own[end:, :] + widened(received[end:, :]))


def split_kernel(level, more, *refs):
    radix, digit = 1 << len(level), digit_of(level)
    main, received = refs[0], refs[1 : 1 + more]
    sends, keep = refs[1 + more : -1], refs[-1]
    rows, end = sends[0].shape[0] - BIAS_ROWS, main.shape[0] - SUBLANES
    total = main[end:, :]
    for ref in received:
        total = total + widened(ref[end:, :])
    for k in range(radix):
        start = pl.multiple_of((digit ^ k) * rows, 16)
        block = main[pl.ds(start, rows), :]
        for ref in received:
            block = block + ref[pl.ds(start, rows), :].astype(F32)
        if k:
            sends[k - 1][:rows, :] = block.astype(BF16)
            sends[k - 1][rows:, :] = narrowed(total)
        else:
            keep[:rows, :] = block
            keep[rows:, :] = total


def gather_kernel(*refs):
    *received, out = refs
    rows = received[0].shape[0] - BIAS_ROWS
    out[:rows, :] = sum(ref[:rows, :].astype(F32) for ref in received)
    out[rows:, :] = sum(widened(ref[rows:, :]) for ref in received)


def finish_kernel(scale, keep, more, out):
    rows = out.shape[0] - BIAS_ROWS
    total = (keep[...] + more[...]) * scale
    out[:rows, :] = total[:rows].astype(BF16)
    out[rows:, :] = narrowed(total[rows:])


def place_kernel(level, taker, given, *refs):
    radix, digit, core = 1 << len(level), digit_of(level), place_of()[1]
    parts, out = refs[:radix], refs[radix]
    rows = parts[0].shape[0] - BIAS_ROWS
    own = jnp.where(core == taker, given[...], parts[0][...])
    for k in range(radix):
        block = parts[k][...] if k else own
        index = digit ^ k
        out[pl.ds(pl.multiple_of(index * rows, 16), rows), :] = block[:rows]

        @pl.when(index == 0)
        def _():
            out[radix * rows :, :] = block[rows:]


def copy_kernel(source, out):
    out[...] = source[...]


def spread_kernel(steps, level, taker, pieces, *refs):
    count, starts = len(steps), steps[0] == 0
    ends = steps[-1] == steps_of(level)[-1]
    digit, core = digit_of(level), place_of()[1]
    direct, passed, refs = refs[:count], refs[count : 2 * count], refs[2 * count :]
    before, refs = (None, refs) if starts else (refs[0], refs[3:])
    (conv, proj), refs = refs[:2], refs[2:]
    bias_out, (wide_conv, wide_proj, wide_bias, sems) = refs[:-4], refs[-4:]
    bias = jnp.zeros((SUBLANES, LANES), F32) if starts else before[...]
    copies = []

    def send(source, target, *at):
        copies.append(pltpu.make_async_copy(source, target, sems.at[at]))
        copies[-1].start()

    for k, here, there in zip(steps, direct, passed):
        end = here.shape[0] - BIAS_ROWS
        block = jnp.where((core == taker) == (k > 0), here[end:, :], there[end:, :])
        bias = jnp.where((digit ^ k) == 0, widened(block), bias)
    if ends:
        wide_bias[...] = jnp.concatenate([bias[i : i + 1, :] for i in range(SUBLANES)], 1)
        column = 0
        for n, out in enumerate(bias_out):
            send(wide_bias.at[:, column : column + out.shape[1]], out, count, n)
            column += out.shape[1]
    else:
        bias_out[0][...] = bias
    for n, (k, here, there) in enumerate(zip(steps, direct, passed)):
        block = jnp.where((core == taker) == (k > 0), here[...], there[...])
        at = 0
        for piece in range(pieces):
            for wide in (wide_conv, wide_proj):
                height = wide.shape[1] // pieces
                for column in range(0, wide.shape[2], LANES):
                    wide[n, piece * height : (piece + 1) * height, column : column + LANES] = (
                        block[at : at + height].astype(F32)
                    )
                    at += height
        for m, (wide, out) in enumerate(((wide_conv, conv), (wide_proj, proj))):
            height = wide.shape[1]
            start = pl.multiple_of((digit ^ k) * height, 16)
            send(wide.at[n], out.at[pl.ds(start, height), :], n, m)
    for copy in copies:
        copy.wait()


def levels_of(chips):
    count = chips.bit_length() - 1
    bits = list(range(count))
    return [tuple(bits[i : i + 2]) for i in range(0, count, 2)]


def swapped(array):
    chips = count_of_chips()
    return lax.ppermute(array, BOTH, [(i, i ^ 1) for i in range(2 * chips)])


def crossed(array, source, step):
    chips = count_of_chips()
    pairs = [(2 * c + source, 2 * (c ^ step) + 1 - source) for c in range(chips)]
    pairs += [(2 * c + 1 - source, 2 * c + source) for c in range(chips)]
    return lax.ppermute(array, BOTH, pairs)


def summed_everywhere(own, offered, scale, heights, widths, fill):
    chips = count_of_chips()
    levels = levels_of(chips)
    radix, turn = 1 << len(levels[0]), steps_of(levels[0])
    rows = own[0].shape[0] - SUBLANES
    exchanged = [swapped(message) for message in offered]
    keep, send = call(
        first_kernel,
        [held(F32, rows + SUBLANES, LANES), held(BF16, rows + BIAS_ROWS, LANES)],
        (own[0], own[turn[0]], exchanged[0]),
        after=fill(0, ()),
    )
    received = [crossed(send, 0, step_between(levels[0], turn[0]))]
    for k, message in zip(turn[1:], exchanged[1:]):
        (send,) = call(next_kernel, [held(BF16, rows + BIAS_ROWS, LANES)], (own[k], message))
        received.append(crossed(send, 0, step_between(levels[0], k)))
    ready = fill(1, (send,))
    source = 1
    for level in range(1, len(levels)):
        radix = 1 << len(levels[level])
        rows //= radix
        *sends, keep = call(
            functools.partial(split_kernel, levels[level], len(received)),
            [held(BF16, rows + BIAS_ROWS, LANES)] * (radix - 1) + [held(F32, rows + SUBLANES, LANES)],
            (keep, *received),
            after=ready if level == 1 else (),
        )
        if level == 1:
            fill(2, (sends[0],))
        keep = swapped(keep)
        received = [
            crossed(sends[k - 1], source, step_between(levels[level], k))
            for k in steps_of(levels[level])
        ]
        source = 1 - source
    (more,) = call(gather_kernel, [held(F32, rows + SUBLANES, LANES)], received, flops=1000000000)
    (part,) = call(
        functools.partial(finish_kernel, scale),
        [held(BF16, rows + BIAS_ROWS, LANES)],
        (keep, more),
        flops=3000000000,
        after=ready if len(levels) == 1 else (),
    )
    if len(levels) == 1:
        fill(2, (part,))
    for level in reversed(range(len(levels))):
        radix = 1 << len(levels[level])
        crossing = {
            k: crossed(part, source, step_between(levels[level], k)) for k in steps_of(levels[level])
        }
        given = swapped(part)
        parts = [part] + [crossing[k] for k in range(1, radix)]
        if level:
            rows = part.shape[0] - BIAS_ROWS
            (part,) = call(
                functools.partial(place_kernel, levels[level], 1 - source),
                [held(BF16, radix * rows + BIAS_ROWS, LANES)],
                (given, *parts),
                after=fill(3, ()) if level == 1 else (),
            )
            source = 1 - source
    taker, pieces = 1 - source, chips // radix
    whole = [shape(F32, chips * h, w) for h, w in zip(heights, widths)]

    def room(count):
        return [
            *[pltpu.VMEM((count, pieces * h, w), F32) for h, w in zip(heights, widths)],
            pltpu.VMEM((1, SUBLANES * LANES), F32),
            pltpu.SemaphoreType.DMA((count + 1, 2)),
        ]

    def spread(steps, forwarded, state):
        ends = steps[-1] == turn[-1]
        biases = [shape(F32, 1, w) for w in widths] if ends else [held(F32, SUBLANES, LANES)]
        at = 2 * len(steps) + 1
        conv, proj, *bias = call(
            functools.partial(spread_kernel, steps, levels[0], taker, pieces),
            whole + biases,
            (*[parts[k] for k in steps], *forwarded, *state),
            scratch=room(len(steps)),
            far=(-1, -2, -3, -4, at, at + 1) if ends else (-1, -2, at, at + 1),
            alias={at: 0, at + 1: 1} if state else None,
        )
        return (*bias, conv, proj)

    state = spread([0], [given], ())
    forwarded = []
    for k in turn:
        message = parts[k]
        after = ()
        if k == turn[0]:
            after = fill(4, ())
        if k == turn[-2:][0]:
            after = (*after, state[0])
        if after:
            (message,) = call(copy_kernel, [held(BF16, *message.shape)], (message,), after=after)
        forwarded.append(swapped(message))
    if len(turn) > 1:
        state = spread(turn[:-1], forwarded[:-1], state)
    conv_bias, proj_bias, conv, proj = spread(turn[-1:], forwarded[-1:], state)
    return conv, proj, conv_bias, proj_bias


def local(signal, conv_weight, conv_bias, out_weight, out_bias, cotangent):
    rows, channels = signal.shape[1:]
    wide = 2 * channels
    late = rows - SPAN
    size = lax.axis_size("tm")
    chips = count_of_chips()
    level = levels_of(chips)[0]
    radix = 1 << len(level)
    widths = (wide, channels)
    heights = [piece_height(n, chips) for n in (TAPS * channels, channels)]
    piece = chips // radix * sum(h * w // LANES for h, w in zip(heights, widths))

    history = [
        lax.ppermute(
            signal[0, rows - n * STEP : rows - n * STEP + STEP],
            "tm",
            [(i, (i + 1) % size) for i in range(size)],
        )
        for n in range(1, TAPS)
    ]
    x, weight, proj_weight, cot, preact, dmixed, mixed_late, dpre_late, conv, proj, bias = call(
        late_kernel,
        [
            held(BF16, rows, channels), held(BF16, TAPS * channels, wide), held(BF16, channels, channels),
            held(BF16, rows, channels),
            held(F32, SPAN, wide), held(F32, SPAN, channels), held(BF16, late, channels),
            held(BF16, late, wide), held(F32, TAPS * channels, wide), held(F32, channels, channels),
            held(F32, SUBLANES, wide + channels),
        ],
        (signal[0], conv_weight, conv_bias.reshape(1, -1), out_weight, cotangent[0]),
        scratch=[pltpu.SemaphoreType.DMA((4,))],
        far=(0, 1, 3, 4),
    )
    grads = [held(F32, TAPS * channels, wide), held(F32, channels, channels)]
    mixed_middle, dpre_middle, conv, proj, bias = call(
        functools.partial(middle_kernel, STEP),
        [held(BF16, STEP, channels), held(BF16, STEP, wide), *grads, held(F32, SUBLANES, wide + channels)],
        (history[0], x, weight, cot, preact, dmixed, conv, proj, bias),
    )
    mixed_early, dpre_early, *pieces = call(
        functools.partial(early_kernel, level, chips),
        [held(BF16, STEP, channels), held(BF16, STEP, wide)]
        + [held(F32, piece + SUBLANES, LANES)] * radix
        + [held(BF16, piece + BIAS_ROWS, LANES)] * (radix - 1),
        (*history, x, weight, cot, preact, dmixed, conv, proj, bias),
        scratch=[pltpu.VMEM((chips * h, w), F32) for h, w in zip(heights, widths)],
    )
    results = {}

    def fill(stage, after):
        if stage == 0:
            (results["back"],) = call(
                back_kernel, [held(BF16, SPAN, channels)], (dpre_early, dpre_middle, weight), after=after
            )
            results["relayed"] = lax.ppermute(results["back"], BOTH, relay_pairs())
            return (results["back"],)
        if stage == 1:
            results["output"], results["partial"], token = call(
                own_kernel,
                [shape(BF16, rows, channels), held(F32, rows, channels), TOKEN],
                (
                    x, weight, proj_weight, out_bias.reshape(1, -1), cot,
                    mixed_early, mixed_middle, mixed_late, dpre_early, dpre_middle, dpre_late,
                ),
                after=after,
            )
            return (token,)
        if stage == 2:
            (onward,) = call(
                relay_kernel,
                [held(BF16, SPAN, channels)],
                (results["back"], results["relayed"]),
                after=after,
            )
            results["incoming"] = lax.ppermute(onward, "tm", plane_pairs())
            return ()
        if stage == 3:
            return (results["incoming"],)
        results["grad_signal"], token = call(
            join_kernel,
            [shape(BF16, rows, channels), TOKEN],
            (results["partial"], results["incoming"]),
        )
        return (token,)

    scale = float(signal.shape[0] * lax.axis_size("run") * rows * size) ** -0.5
    grad_conv, grad_proj, grad_cbias, grad_pbias = summed_everywhere(
        pieces[:radix], pieces[radix:], scale, heights, widths, fill
    )
    return (
        results["output"][None],
        results["grad_signal"][None],
        grad_conv[: TAPS * channels],
        grad_cbias[0],
        grad_proj[:channels],
        grad_pbias[0],
    )


def solution(mesh):
    placed = (P("run", "tm", None), P(), P(), P(), P(), P("run", "tm", None))
    return jax.shard_map(
        local,
        mesh=mesh,
        in_specs=placed,
        out_specs=(P("run", "tm", None), P("run", "tm", None), P(), P(), P(), P()),
        check_vma=False,
    )
```

```python
import functools

import jax
import jax.numpy as jnp
from jax import lax
from jax.experimental import pallas as pl
from jax.experimental.pallas import tpu as pltpu
from jax.sharding import PartitionSpec as P

STEP = 256
TAPS = 3
SPAN = (TAPS - 1) * STEP
BOTH = ("tm", "run")
LANES = 128
SUBLANES = 8
BIAS_ROWS = 2 * SUBLANES
F32 = jnp.float32
BF16 = jnp.bfloat16
VMEM = pl.BlockSpec(memory_space=pltpu.VMEM)
ANY = pl.BlockSpec(memory_space=pl.ANY)
HBM = pl.BlockSpec(memory_space=pltpu.HBM)
MIB = 1024 * 1024


def call(kernel, out_shape, args, flops=0, scratch=(), after=(), far=(), alias=None):
    moved = sum(a.size * a.dtype.itemsize for a in args)
    inner = kernel
    if after:
        count = len(args)
        inner = lambda *refs: kernel(*refs[:count], *refs[count + len(after) :])
    ins = [HBM if i in far else VMEM for i in range(len(args))]
    outs = [HBM if -1 - i in far else VMEM for i in range(len(out_shape))]
    placed = [
        pltpu.with_memory_space_constraint(a, pltpu.HBM if i in far else pltpu.VMEM)
        for i, a in enumerate(args)
    ]
    return pl.pallas_call(
        inner,
        out_shape=out_shape,
        in_specs=ins + [ANY] * len(after),
        out_specs=outs,
        scratch_shapes=list(scratch),
        input_output_aliases=alias or {},
        cost_estimate=pl.CostEstimate(flops=flops, bytes_accessed=8, transcendentals=0),
        compiler_params=pltpu.CompilerParams(vmem_limit_bytes=(8 if count_of_chips() <= 16 else 40) * MIB),
    )(*placed, *after)


def held(dtype, *dims):
    return pltpu.VMEM(dims, dtype)


def shape(dtype, *dims):
    return jax.ShapeDtypeStruct(dims, dtype)


def count_of_chips():
    return lax.axis_size("tm") * lax.axis_size("run") // 2


def place_of():
    flat = lax.axis_index("tm") * lax.axis_size("run") + lax.axis_index("run")
    return flat // 2, lax.rem(flat, 2)


def digit_of(level):
    chip = place_of()[0]
    return sum(lax.rem(chip // (1 << bit), 2) * (1 << i) for i, bit in enumerate(level))


def steps_of(level):
    last = (1 << len(level)) - 1
    return [last, *range(1, last)]


def step_between(level, k):
    return sum(1 << bit for i, bit in enumerate(level) if k >> i & 1)


TOKEN = held(F32, SUBLANES, LANES)


def dot(a, b):
    return jnp.dot(a, b, preferred_element_type=F32)


def dot_rows(a, b):
    return lax.dot_general(a, b, (((0,), (0,)), ((), ())), preferred_element_type=F32)


def dot_columns(a, b):
    return lax.dot_general(a, b, (((1,), (1,)), ((), ())), preferred_element_type=F32)


def gates(preact, dmixed):
    channels = dmixed.shape[1]
    filtered = jnp.tanh(preact[:, :channels])
    gated = jax.nn.sigmoid(preact[:, channels:])
    mixed = filtered * gated
    dfiltered = dmixed * gated * (1.0 - filtered * filtered)
    dgated = dmixed * mixed * (1.0 - gated)
    return mixed.astype(BF16), dfiltered.astype(BF16), dgated.astype(BF16)


def late_kernel(
    signal_in, weight_in, bias, out_weight_in, cot_in,
    signal, weight, out_weight, cot,
    preact_out, dmixed_out, mixed_out, dpre_out, grad_conv, grad_proj, grad_bias, sems,
):
    rows, channels = signal.shape
    pairs = ((signal_in, signal), (weight_in, weight), (cot_in, cot), (out_weight_in, out_weight))
    copies = [pltpu.make_async_copy(a, b, sems.at[i]) for i, (a, b) in enumerate(pairs)]
    for copy in copies:
        copy.start()
    tap = lambda k: weight[k * channels : (k + 1) * channels, :]
    copies[0].wait()
    copies[1].wait()
    preact_out[...] = dot(signal[:SPAN, :], tap(0)) + bias[...]
    for k in range(1, TAPS - 1):
        preact_out[k * STEP :, :] += dot(signal[: SPAN - k * STEP, :], tap(k))
    copies[2].wait()
    copies[3].wait()
    dmixed_out[...] = dot_columns(cot[:SPAN, :], out_weight[...])
    for begin in range(SPAN, rows, STEP):
        here = slice(begin, begin + STEP)
        at = slice(begin - SPAN, begin - SPAN + STEP)
        preact = bias[...]
        for k in range(TAPS):
            preact = preact + dot(signal[begin - k * STEP : begin - k * STEP + STEP, :], tap(k))
        mixed, dfiltered, dgated = gates(preact, dot_columns(cot[here, :], out_weight[...]))
        mixed_out[at, :] = mixed
        dpre_out[at, :channels] = dfiltered
        dpre_out[at, channels:] = dgated
    dpre = dpre_out[...]
    for k in range(TAPS):
        grad_conv[k * channels : (k + 1) * channels, :] = dot_rows(
            signal[SPAN - k * STEP : rows - k * STEP, :], dpre
        )
    grad_proj[...] = dot_rows(mixed_out[...], cot[SPAN:, :])
    ones = jnp.ones((BIAS_ROWS, rows), BF16)
    grad_bias[:, : 2 * channels] = dot(ones[:, : rows - SPAN], dpre)[:SUBLANES]
    grad_bias[:, 2 * channels :] = dot(ones, cot[...])[:SUBLANES]


def chunk(begin, taps, past, signal, weight, cot, preact_in, dmixed_in, conv_in, proj_in, bias_in, mixed_out, dpre_out, conv, proj):
    channels = signal.shape[1]
    here = slice(begin, begin + STEP)
    own = begin // STEP + 1
    past = [
        jnp.where(lax.axis_index("tm") == 0, jnp.zeros_like(block), block[...]) for block in past
    ]
    preact = preact_in[here, :]
    for k in taps:
        preact = preact + dot(past[k - own], weight[k * channels : (k + 1) * channels, :])
    mixed, dfiltered, dgated = gates(preact, dmixed_in[here, :])
    mixed_out[...] = mixed
    dpre_out[:, :channels] = dfiltered
    dpre_out[:, channels:] = dgated
    dpre = dpre_out[...]
    for k in range(TAPS):
        at = slice(k * channels, (k + 1) * channels)
        seen = past[k - own] if k >= own else signal[begin - k * STEP : begin - k * STEP + STEP, :]
        conv[at, :] = conv_in[at, :] + dot_rows(seen, dpre)
    proj[: channels, :] = proj_in[...] + dot_rows(mixed, cot[here, :])
    columns = dot(jnp.ones((BIAS_ROWS, STEP), BF16), dpre)[:SUBLANES]
    return jnp.concatenate([bias_in[:, : 2 * channels] + columns, bias_in[:, 2 * channels :]], 1)


def middle_kernel(begin, *refs):
    *ins, grad_bias, ahead = refs
    near, signal, weight, _, preact_in = ins[:5]
    grad_bias[...] = chunk(begin, range(begin // STEP + 1, TAPS), ins[:1], *ins[1:])
    channels = signal.shape[1]
    block = jnp.where(lax.axis_index("tm") == 0, jnp.zeros_like(near), near[...])
    ahead[...] = preact_in[:STEP, :] + dot(block, weight[channels : 2 * channels, :])


def early_kernel(level, pieces, *refs):
    radix, digit, core = 1 << len(level), digit_of(level), place_of()[1]
    turn = steps_of(level)
    ins, (mixed_out, dpre_out), refs = refs[: TAPS + 7], refs[TAPS + 7 : TAPS + 9], refs[TAPS + 9 :]
    own, offered = refs[:radix], refs[radix : 2 * radix - 1]
    grad_conv, grad_proj = refs[2 * radix - 1 :]
    bias = chunk(0, range(2, TAPS), ins[: TAPS - 1], *ins[TAPS - 1 :], mixed_out, dpre_out, grad_conv, grad_proj)
    conv_in, proj_in = ins[-3], ins[-2]
    for grad, filled in ((grad_conv, conv_in.shape[0]), (grad_proj, proj_in.shape[0])):
        if filled < grad.shape[0]:
            grad[filled:, :] = jnp.zeros((grad.shape[0] - filled, grad.shape[1]), F32)
    lines = [bias[:1, c : c + LANES] for c in range(0, bias.shape[1], LANES)]
    lines += [jnp.zeros((1, LANES), F32)] * (SUBLANES - len(lines))
    bias = jnp.concatenate(lines, 0)

    def pack(k, target, kind):
        at = 0
        for piece in range(pieces // radix):
            index = (digit ^ k) * (pieces // radix) + piece
            for grad in (grad_conv, grad_proj):
                height = grad.shape[0] // pieces
                begin = pl.multiple_of(index * height, 16)
                for column in range(0, grad.shape[1], LANES):
                    target[at : at + height, :] = grad[
                        pl.ds(begin, height), column : column + LANES
                    ].astype(kind)
                    at += height
        target[at:, :] = bias if kind == F32 else narrowed(bias)

    @pl.when(core == 0)
    def _():
        pack(0, offered[0], BF16)
        for k in turn:
            pack(k, own[k], F32)

    @pl.when(core == 1)
    def _():
        for k, target in zip(turn, offered):
            pack(k, target, BF16)
        pack(0, own[0], F32)


def back_kernel(*refs):
    *blocks, weight, out = refs
    channels = out.shape[1]
    tap = lambda k: weight[k * channels : (k + 1) * channels, :]
    for n in range(TAPS - 1):
        total = dot_columns(blocks[n][...], tap(TAPS - 1))
        for k in range(TAPS - 1 - n, TAPS - 1):
            total = total + dot_columns(blocks[n - TAPS + 1 + k][...], tap(k))
        out[n * STEP : (n + 1) * STEP, :] = total.astype(BF16)


def own_kernel(signal, weight, out_weight, out_bias, cot, *refs):
    rows, channels = signal.shape
    tap = lambda k: weight[k * channels : (k + 1) * channels, :]
    mixed, dpre, (output, partial, token) = refs[:TAPS], refs[TAPS : 2 * TAPS], refs[2 * TAPS :]
    token[...] = jnp.zeros_like(token)

    def part(refs, begin):
        block = min(begin // STEP, TAPS - 1)
        return refs[block][begin - block * STEP : begin - block * STEP + STEP, :]

    for begin in range(0, rows, STEP):
        here = slice(begin, begin + STEP)
        hidden = dot(part(mixed, begin), out_weight[...]) + out_bias[...]
        output[here, :] = (signal[here, :].astype(F32) + hidden).astype(BF16)
        total = cot[here, :].astype(F32)
        for k in range(TAPS):
            if begin + k * STEP < rows:
                total = total + dot_columns(part(dpre, begin + k * STEP), tap(k))
        partial[here, :] = total


PLANE = 4


def relay_pairs():
    runs, size = lax.axis_size("run"), lax.axis_size("tm")
    pairs = []
    for t in range(size):
        for r in range(runs):
            to = ((t - PLANE) % size) * runs + r if t % PLANE == 0 else t * runs + (r ^ 1)
            pairs.append((t * runs + r, to))
    return pairs


def plane_pairs():
    size = lax.axis_size("tm")
    return [(t, t - 1 if t % PLANE else t + PLANE - 1) for t in range(size)]


def relay_kernel(back, relayed, onward):
    first = lax.rem(lax.axis_index("tm"), PLANE) == 0
    onward[...] = jnp.where(first, relayed[...], back[...])


def join_kernel(partial, incoming, out, token):
    token[...] = jnp.zeros_like(token)
    rows = partial.shape[0]
    last = lax.axis_index("tm") == lax.axis_size("tm") - 1
    out[: rows - SPAN, :] = partial[: rows - SPAN, :].astype(BF16)
    more = jnp.where(last, jnp.zeros(incoming.shape, F32), incoming[...].astype(F32))
    out[rows - SPAN :, :] = (partial[rows - SPAN :, :] + more).astype(BF16)


def piece_height(rows, pieces):
    return -(-rows // (pieces * 16)) * 16


def widened(block):
    wide = block.astype(F32)
    return wide[:SUBLANES] + wide[SUBLANES:]


def narrowed(total):
    high = total.astype(BF16).astype(F32)
    return jnp.concatenate([high, total - high], 0).astype(BF16)


def first_kernel(keep_own, send_own, received, keep, send):
    end = send.shape[0] - BIAS_ROWS
    more, bias = received[:end, :].astype(F32), widened(received[end:, :])
    keep[:end, :] = keep_own[:end, :] + more
    keep[end:, :] = keep_own[end:, :] + bias
    send[:end, :] = (send_own[:end, :] + more).astype(BF16)
    send[end:, :] = narrowed(send_own[end:, :] + bias)


def next_kernel(send_own, received, send):
    end = send.shape[0] - BIAS_ROWS
    send[:end, :] = (send_own[:end, :] + received[:end, :].astype(F32)).astype(BF16)
    send[end:, :] = narrowed(send_own[end:, :] + widened(received[end:, :]))


def split_kernel(level, more, *refs):
    radix, digit = 1 << len(level), digit_of(level)
    main, received = refs[0], refs[1 : 1 + more]
    sends, keep = refs[1 + more : -1], refs[-1]
    rows, end = sends[0].shape[0] - BIAS_ROWS, main.shape[0] - SUBLANES
    total = main[end:, :]
    for ref in received:
        total = total + widened(ref[end:, :])
    for k in range(radix):
        start = pl.multiple_of((digit ^ k) * rows, 16)
        block = main[pl.ds(start, rows), :]
        for ref in received:
            block = block + ref[pl.ds(start, rows), :].astype(F32)
        if k:
            sends[k - 1][:rows, :] = block.astype(BF16)
            sends[k - 1][rows:, :] = narrowed(total)
        else:
            keep[:rows, :] = block
            keep[rows:, :] = total


def gather_kernel(*refs):
    *received, out = refs
    rows = received[0].shape[0] - BIAS_ROWS
    out[:rows, :] = sum(ref[:rows, :].astype(F32) for ref in received)
    out[rows:, :] = sum(widened(ref[rows:, :]) for ref in received)


def finish_kernel(scale, keep, more, out):
    rows = out.shape[0] - BIAS_ROWS
    total = (keep[...] + more[...]) * scale
    out[:rows, :] = total[:rows].astype(BF16)
    out[rows:, :] = narrowed(total[rows:])


def place_kernel(level, taker, given, *refs):
    radix, digit, core = 1 << len(level), digit_of(level), place_of()[1]
    parts, out = refs[:radix], refs[radix]
    rows = parts[0].shape[0] - BIAS_ROWS
    own = jnp.where(core == taker, given[...], parts[0][...])
    for k in range(radix):
        block = parts[k][...] if k else own
        index = digit ^ k
        out[pl.ds(pl.multiple_of(index * rows, 16), rows), :] = block[:rows]

        @pl.when(index == 0)
        def _():
            out[radix * rows :, :] = block[rows:]


def copy_kernel(source, out):
    out[...] = source[...]


def spread_kernel(steps, level, taker, pieces, *refs):
    count, starts = len(steps), steps[0] == 0
    ends = steps[-1] == steps_of(level)[-1]
    digit, core = digit_of(level), place_of()[1]
    direct, passed, refs = refs[:count], refs[count : 2 * count], refs[2 * count :]
    before, refs = (None, refs) if starts else (refs[0], refs[3:])
    (conv, proj), refs = refs[:2], refs[2:]
    bias_out, (wide_conv, wide_proj, wide_bias, sems) = refs[:-4], refs[-4:]
    bias = jnp.zeros((SUBLANES, LANES), F32) if starts else before[...]
    copies = []

    def send(source, target, *at):
        copies.append(pltpu.make_async_copy(source, target, sems.at[at]))
        copies[-1].start()

    for k, here, there in zip(steps, direct, passed):
        end = here.shape[0] - BIAS_ROWS
        block = jnp.where((core == taker) == (k > 0), here[end:, :], there[end:, :])
        bias = jnp.where((digit ^ k) == 0, widened(block), bias)
    if ends:
        wide_bias[...] = jnp.concatenate([bias[i : i + 1, :] for i in range(SUBLANES)], 1)
        column = 0
        for n, out in enumerate(bias_out):
            send(wide_bias.at[:, column : column + out.shape[1]], out, count, n)
            column += out.shape[1]
    else:
        bias_out[0][...] = bias
    for n, (k, here, there) in enumerate(zip(steps, direct, passed)):
        block = jnp.where((core == taker) == (k > 0), here[...], there[...])
        at = 0
        for piece in range(pieces):
            for wide in (wide_conv, wide_proj):
                height = wide.shape[1] // pieces
                for column in range(0, wide.shape[2], LANES):
                    wide[n, piece * height : (piece + 1) * height, column : column + LANES] = (
                        block[at : at + height].astype(F32)
                    )
                    at += height
        for m, (wide, out) in enumerate(((wide_conv, conv), (wide_proj, proj))):
            height = wide.shape[1]
            start = pl.multiple_of((digit ^ k) * height, 16)
            send(wide.at[n], out.at[pl.ds(start, height), :], n, m)
    for copy in copies:
        copy.wait()


def levels_of(chips):
    count = chips.bit_length() - 1
    bits = list(range(count))
    return [tuple(bits[i : i + 2]) for i in range(0, count, 2)]


def swapped(array):
    chips = count_of_chips()
    return lax.ppermute(array, BOTH, [(i, i ^ 1) for i in range(2 * chips)])


def crossed(array, source, step):
    chips = count_of_chips()
    pairs = [(2 * c + source, 2 * (c ^ step) + 1 - source) for c in range(chips)]
    pairs += [(2 * c + 1 - source, 2 * c + source) for c in range(chips)]
    return lax.ppermute(array, BOTH, pairs)


def summed_everywhere(own, offered, scale, heights, widths, fill):
    chips = count_of_chips()
    levels = levels_of(chips)
    radix, turn = 1 << len(levels[0]), steps_of(levels[0])
    rows = own[0].shape[0] - SUBLANES
    exchanged = [swapped(message) for message in offered]
    keep, send = call(
        first_kernel,
        [held(F32, rows + SUBLANES, LANES), held(BF16, rows + BIAS_ROWS, LANES)],
        (own[0], own[turn[0]], exchanged[0]),
        after=fill(0, ()),
    )
    received = [crossed(send, 0, step_between(levels[0], turn[0]))]
    for k, message in zip(turn[1:], exchanged[1:]):
        (send,) = call(next_kernel, [held(BF16, rows + BIAS_ROWS, LANES)], (own[k], message))
        received.append(crossed(send, 0, step_between(levels[0], k)))
    ready = fill(1, (send,))
    source = 1
    for level in range(1, len(levels)):
        radix = 1 << len(levels[level])
        rows //= radix
        *sends, keep = call(
            functools.partial(split_kernel, levels[level], len(received)),
            [held(BF16, rows + BIAS_ROWS, LANES)] * (radix - 1) + [held(F32, rows + SUBLANES, LANES)],
            (keep, *received),
            after=ready if level == 1 else (),
        )
        if level == 1:
            fill(2, (sends[0],))
        keep = swapped(keep)
        received = [
            crossed(sends[k - 1], source, step_between(levels[level], k))
            for k in steps_of(levels[level])
        ]
        source = 1 - source
    (more,) = call(gather_kernel, [held(F32, rows + SUBLANES, LANES)], received, flops=1000000000)
    (part,) = call(
        functools.partial(finish_kernel, scale),
        [held(BF16, rows + BIAS_ROWS, LANES)],
        (keep, more),
        flops=3000000000,
        after=ready if len(levels) == 1 else (),
    )
    if len(levels) == 1:
        fill(2, (part,))
    for level in reversed(range(len(levels))):
        radix = 1 << len(levels[level])
        crossing = {
            k: crossed(part, source, step_between(levels[level], k)) for k in steps_of(levels[level])
        }
        given = swapped(part)
        parts = [part] + [crossing[k] for k in range(1, radix)]
        if level:
            rows = part.shape[0] - BIAS_ROWS
            (part,) = call(
                functools.partial(place_kernel, levels[level], 1 - source),
                [held(BF16, radix * rows + BIAS_ROWS, LANES)],
                (given, *parts),
                after=fill(3, ()) if level == 1 else (),
            )
            source = 1 - source
    taker, pieces = 1 - source, chips // radix
    whole = [shape(F32, chips * h, w) for h, w in zip(heights, widths)]

    def room(count):
        return [
            *[pltpu.VMEM((count, pieces * h, w), F32) for h, w in zip(heights, widths)],
            pltpu.VMEM((1, SUBLANES * LANES), F32),
            pltpu.SemaphoreType.DMA((count + 1, 2)),
        ]

    def spread(steps, forwarded, state):
        ends = steps[-1] == turn[-1]
        biases = [shape(F32, 1, w) for w in widths] if ends else [held(F32, SUBLANES, LANES)]
        at = 2 * len(steps) + 1
        conv, proj, *bias = call(
            functools.partial(spread_kernel, steps, levels[0], taker, pieces),
            whole + biases,
            (*[parts[k] for k in steps], *forwarded, *state),
            scratch=room(len(steps)),
            far=(-1, -2, -3, -4, at, at + 1) if ends else (-1, -2, at, at + 1),
            alias={at: 0, at + 1: 1} if state else None,
        )
        return (*bias, conv, proj)

    state = spread([0], [given], ())
    forwarded = []
    for k in turn:
        message = parts[k]
        after = ()
        if k == turn[0]:
            after = fill(4, ())
        if k == turn[-2:][0]:
            after = (*after, state[0])
        if after:
            (message,) = call(copy_kernel, [held(BF16, *message.shape)], (message,), after=after)
        forwarded.append(swapped(message))
    if len(turn) > 1:
        state = spread(turn[:-1], forwarded[:-1], state)
    conv_bias, proj_bias, conv, proj = spread(turn[-1:], forwarded[-1:], state)
    return conv, proj, conv_bias, proj_bias


def local(signal, conv_weight, conv_bias, out_weight, out_bias, cotangent):
    rows, channels = signal.shape[1:]
    wide = 2 * channels
    late = rows - SPAN
    size = lax.axis_size("tm")
    chips = count_of_chips()
    level = levels_of(chips)[0]
    radix = 1 << len(level)
    widths = (wide, channels)
    heights = [piece_height(n, chips) for n in (TAPS * channels, channels)]
    piece = chips // radix * sum(h * w // LANES for h, w in zip(heights, widths))

    history = [
        lax.ppermute(
            signal[0, rows - n * STEP : rows - n * STEP + STEP],
            "tm",
            [(i, (i + 1) % size) for i in range(size)],
        )
        for n in range(1, TAPS)
    ]
    x, weight, proj_weight, cot, preact, dmixed, mixed_late, dpre_late, conv, proj, bias = call(
        late_kernel,
        [
            held(BF16, rows, channels), held(BF16, TAPS * channels, wide), held(BF16, channels, channels),
            held(BF16, rows, channels),
            held(F32, SPAN, wide), held(F32, SPAN, channels), held(BF16, late, channels),
            held(BF16, late, wide), held(F32, TAPS * channels, wide), held(F32, channels, channels),
            held(F32, SUBLANES, wide + channels),
        ],
        (signal[0], conv_weight, conv_bias.reshape(1, -1), out_weight, cotangent[0]),
        scratch=[pltpu.SemaphoreType.DMA((4,))],
        far=(0, 1, 3, 4),
    )
    grads = [held(F32, TAPS * channels, wide), held(F32, channels, channels)]
    mixed_middle, dpre_middle, conv, proj, bias, ahead = call(
        functools.partial(middle_kernel, STEP),
        [held(BF16, STEP, channels), held(BF16, STEP, wide), *grads, held(F32, SUBLANES, wide + channels), held(F32, STEP, wide)],
        (history[0], x, weight, cot, preact, dmixed, conv, proj, bias),
    )
    mixed_early, dpre_early, *pieces = call(
        functools.partial(early_kernel, level, chips),
        [held(BF16, STEP, channels), held(BF16, STEP, wide)]
        + [held(F32, piece + SUBLANES, LANES)] * radix
        + [held(BF16, piece + BIAS_ROWS, LANES)] * (radix - 1),
        (*history, x, weight, cot, ahead, dmixed, conv, proj, bias),
        scratch=[pltpu.VMEM((chips * h, w), F32) for h, w in zip(heights, widths)],
    )
    results = {}

    def fill(stage, after):
        if stage == 0:
            (results["back"],) = call(
                back_kernel, [held(BF16, SPAN, channels)], (dpre_early, dpre_middle, weight), after=after
            )
            results["relayed"] = lax.ppermute(results["back"], BOTH, relay_pairs())
            return (results["back"],)
        if stage == 1:
            results["output"], results["partial"], token = call(
                own_kernel,
                [shape(BF16, rows, channels), held(F32, rows, channels), TOKEN],
                (
                    x, weight, proj_weight, out_bias.reshape(1, -1), cot,
                    mixed_early, mixed_middle, mixed_late, dpre_early, dpre_middle, dpre_late,
                ),
                after=after,
            )
            return (token,)
        if stage == 2:
            (onward,) = call(
                relay_kernel,
                [held(BF16, SPAN, channels)],
                (results["back"], results["relayed"]),
                after=after,
            )
            results["incoming"] = lax.ppermute(onward, "tm", plane_pairs())
            return ()
        if stage == 3:
            return (results["incoming"],)
        results["grad_signal"], token = call(
            join_kernel,
            [shape(BF16, rows, channels), TOKEN],
            (results["partial"], results["incoming"]),
        )
        return (token,)

    scale = float(signal.shape[0] * lax.axis_size("run") * rows * size) ** -0.5
    grad_conv, grad_proj, grad_cbias, grad_pbias = summed_everywhere(
        pieces[:radix], pieces[radix:], scale, heights, widths, fill
    )
    return (
        results["output"][None],
        results["grad_signal"][None],
        grad_conv[: TAPS * channels],
        grad_cbias[0],
        grad_proj[:channels],
        grad_pbias[0],
    )


def solution(mesh):
    placed = (P("run", "tm", None), P(), P(), P(), P(), P("run", "tm", None))
    return jax.shard_map(
        local,
        mesh=mesh,
        in_specs=placed,
        out_specs=(P("run", "tm", None), P("run", "tm", None), P(), P(), P(), P()),
        check_vma=False,
    )
```
